32 devices in a mesh: dp: 4 (over z), mp: 8 (over y, x, core).
Axes of the slice: x: 2, y: 2, z: 4, core: 2. Of those that a mesh axis runs over, the one named last changes fastest.
Arguments:
- tokens: bfloat16 [32768, 2048], P(('dp', 'mp')), may hold values from -6 to 6
- cotangent: bfloat16 [32768, 2048], P(('dp', 'mp')), may hold values from -0.015625 to 0.015625
- lengths: int32 [4], P('dp'), may hold values from 1024 to 8192, as said below
- inner_weight: float32 [2048, 64, 128], P('dp', 'mp'), may hold values from -0.125 to 0.125
- step_weight: float32 [2048, 64], P('dp', 'mp'), may hold values from -0.0625 to 0.0625
- state_weight: float32 [2048, 256], P('dp'), may hold values from -0.125 to 0.125
- output_weight: float32 [2048, 4096], P('dp', 'mp'), may hold values from -0.09375 to 0.09375
- inner_filter: float32 [5, 4096], P(None, 'mp'), may hold values from -3 to 3
- state_filter: float32 [5, 256], replicated, may hold values from -3 to 3
- head_params: float32 [3, 64], P(None, 'mp'), may hold values from -4 to 2.5
- norm_gain: float32 [4096], P('mp'), may hold values from 0.5 to 1.5
- inner_moments: float32 [2, 2048, 64, 128], P(None, 'dp', 'mp'), as said below
- step_moments: float32 [2, 2048, 64], P(None, 'dp', 'mp'), as said below
- state_moments: float32 [2, 2048, 256], P(None, 'dp'), as said below
- output_moments: float32 [2, 2048, 4096], P(None, 'dp', 'mp'), as said below
- inner_filter_moments: float32 [2, 5, 4096], P(None, None, 'mp'), as said below
- state_filter_moments: float32 [2, 5, 256], replicated, as said below
- head_moments: float32 [2, 3, 64], P(None, None, 'mp'), as said below
- gain_moments: float32 [2, 4096], P(None, 'mp'), as said below
Outputs:
- mixed: bfloat16 [32768, 2048], P(('dp', 'mp'))
- tokens_gradient: bfloat16 [32768, 2048], P(('dp', 'mp'))
- inner_gradient: float32 [2048, 64, 128], P('dp', 'mp')
- step_gradient: float32 [2048, 64], P('dp', 'mp')
- state_gradient: float32 [2048, 256], P('dp')
- output_gradient: float32 [2048, 4096], P('dp', 'mp')
- inner_filter_gradient: float32 [5, 4096], P(None, 'mp')
- state_filter_gradient: float32 [5, 256], replicated
- head_gradient: float32 [3, 64], P(None, 'mp')
- gain_gradient: float32 [4096], P('mp')
- inner_update: float32 [3, 2048, 64, 128], P(None, 'dp', 'mp')
- step_update: float32 [3, 2048, 64], P(None, 'dp', 'mp')
- state_update: float32 [3, 2048, 256], P(None, 'dp')
- output_update: float32 [3, 2048, 4096], P(None, 'dp', 'mp')
- inner_filter_update: float32 [3, 5, 4096], P(None, None, 'mp')
- state_filter_update: float32 [3, 5, 256], replicated
- head_update: float32 [3, 3, 64], P(None, None, 'mp')
- gain_update: float32 [3, 4096], P(None, 'mp')
The draws below stay inside these ranges and needn't reach their ends.
Inputs may be any that keep to these rules, and one draw needn't show every extreme that they name: `lengths`: one sequence in every draw has all 8192 positions valid. `inner_moments`: row 1 (second moments) is positive. `step_moments`: row 1 (second moments) is positive. `state_moments`: row 1 (second moments) is positive. `output_moments`: row 1 (second moments) is positive. `inner_filter_moments`: row 1 (second moments) is positive. `state_filter_moments`: row 1 (second moments) is positive. `head_moments`: row 1 (second moments) is positive. `gain_moments`: row 1 (second moments) is positive.
All inputs are finite; a program needn't handle non-finite values.
Results may differ from the reference program's by a relative error of at most 0.012.
Values may be sent and summed in bfloat16 or wider, within the bound.
No kernel may reach another device: no remote copies, remote signals or barrier semaphores. Data moves between devices by JAX's collectives and lax.ppermute only.
A program may use at most 576 MiB of HBM per device.

```python
import math
import jax
import jax.numpy as jnp
from jax import lax

D = 2048
HEADS = 64
HEAD_DIM = 64
STATE = 128
CONV = 4
BLOCK = 256
STEP = 100
SEQ_LEN = 8192
INNER = 4096
SEQS = 4
TOKENS = 32768


def draw_lengths(key, part):
    first_key, second_key = jax.random.split(jax.random.fold_in(key, 11))
    drawn = jax.random.randint(first_key, (SEQS,), SEQ_LEN // 8, SEQ_LEN + 1)
    chosen = jax.random.randint(second_key, (), 0, SEQS)
    return jnp.where(jnp.arange(SEQS) == chosen, SEQ_LEN, drawn).astype(jnp.int32)


def draw_head_params(key, part):
    first_key, second_key, third_key = jax.random.split(jax.random.fold_in(key, 13), 3)
    step_bias = jax.random.uniform(first_key, (HEADS,), jnp.float32, -4.0, -1.0)
    decay_log = jax.random.uniform(second_key, (HEADS,), jnp.float32, -3.0, 2.5)
    skip_coef = jax.random.uniform(third_key, (HEADS,), jnp.float32, 0.5, 1.5)
    return jnp.stack([step_bias, decay_log, skip_coef])


def moment_pair(key, array_shape, tag):
    first_key, second_key = jax.random.split(jax.random.fold_in(key, tag))
    first_moment = jax.random.normal(first_key, array_shape, jnp.float32)
    second_moment = jnp.exp(jax.random.uniform(second_key, array_shape, jnp.float32, math.log(0.25), math.log(4.0)))
    return jnp.stack([first_moment, second_moment])


def draw_inner_moments(key, part):
    return moment_pair(key, (D, HEADS, 2 * HEAD_DIM), 101)


def draw_step_moments(key, part):
    return moment_pair(key, (D, HEADS), 102)


def draw_state_moments(key, part):
    return moment_pair(key, (D, 2 * STATE), 103)


def draw_output_moments(key, part):
    return moment_pair(key, (D, INNER), 104)


def draw_inner_filter_moments(key, part):
    return moment_pair(key, (CONV + 1, INNER), 105)


def draw_state_filter_moments(key, part):
    return moment_pair(key, (CONV + 1, 2 * STATE), 106)


def draw_head_moments(key, part):
    return moment_pair(key, (3, HEADS), 107)


def draw_gain_moments(key, part):
    return moment_pair(key, (INNER,), 108)


def shard_levels(key, dims, cuts, least, largest):
    gain, own = 1.0, jax.random.fold_in(key, 6)
    for position, blocks in cuts:
        draws = jnp.exp(jax.random.uniform(jax.random.fold_in(own, position), (blocks,), jnp.float32, least / len(cuts), largest / len(cuts)))
        gain = gain * jnp.repeat(draws, dims[position] // blocks).reshape([-1 if axis == position else 1 for axis in range(len(dims))])
    return gain


def scatter_about(key, dims, deviation, reach, pieces=(), dtype=jnp.bfloat16):
    level = shard_levels(key, dims, pieces, -0.22, 0.18) if pieces else 1.0
    values = jax.random.normal(key, dims, jnp.float32) * deviation * level
    return jnp.minimum(jnp.maximum(values, -reach), reach).astype(dtype)


def setup_inputs(seed: int = 0) -> dict:
    keys = jax.random.split(jax.random.key(seed), 20)
    return {
        "tokens": scatter_about(keys[0], (TOKENS, D), 1.0, 6.0, ((0, 32),)),
        "cotangent": scatter_about(keys[1], (TOKENS, D), (4 * TOKENS) ** -0.5, 0.015625, ((0, 32),)),
        "lengths": draw_lengths(jax.random.fold_in(keys[19], 71), 0),
        "inner_weight": scatter_about(keys[3], (D, HEADS, 2 * HEAD_DIM), D ** -0.5, 0.125, ((0, 4), (1, 8)), jnp.float32),
        "step_weight": scatter_about(keys[4], (D, HEADS), (4 * D) ** -0.5, 0.0625, ((0, 4), (1, 8)), jnp.float32),
        "state_weight": scatter_about(keys[5], (D, 2 * STATE), D ** -0.5, 0.125, ((0, 4),), jnp.float32),
        "output_weight": scatter_about(keys[6], (D, INNER), INNER ** -0.5, 0.09375, ((0, 4), (1, 8)), jnp.float32),
        "inner_filter": scatter_about(keys[7], (CONV + 1, INNER), 0.5, 3.0, ((1, 8),), jnp.float32),
        "state_filter": scatter_about(keys[8], (CONV + 1, 2 * STATE), 0.5, 3.0, (), jnp.float32),
        "head_params": draw_head_params(jax.random.fold_in(keys[19], 71), 0),
        "norm_gain": jnp.clip(1.0 + 0.1 * jax.random.normal(keys[10], (INNER,), jnp.float32), 0.5, 1.5),
        "inner_moments": draw_inner_moments(jax.random.fold_in(keys[19], 71), 0),
        "step_moments": draw_step_moments(jax.random.fold_in(keys[19], 71), 0),
        "state_moments": draw_state_moments(jax.random.fold_in(keys[19], 71), 0),
        "output_moments": draw_output_moments(jax.random.fold_in(keys[19], 71), 0),
        "inner_filter_moments": draw_inner_filter_moments(jax.random.fold_in(keys[19], 71), 0),
        "state_filter_moments": draw_state_filter_moments(jax.random.fold_in(keys[19], 71), 0),
        "head_moments": draw_head_moments(jax.random.fold_in(keys[19], 71), 0),
        "gain_moments": draw_gain_moments(jax.random.fold_in(keys[19], 71), 0),
    }


@jax.custom_vjp
def low(v):
    return lax.optimization_barrier(v.astype(jnp.bfloat16)).astype(jnp.float32)

@jax.custom_vjp
def low_back(v):
    return v

def low_keep(v):
    return (low(v), None)

def low_pass(kept, grad):
    return (grad,)

def back_keep(v):
    return (v, None)

def back_low(kept, grad):
    return (low(grad),)
low.defvjp(low_keep, low_pass)
low_back.defvjp(back_keep, back_low)
highest = lax.Precision.HIGHEST
eps_norm = 1e-05
beta_one = 0.9
beta_two = 0.95
adam_eps = 1e-08
decay_rate = 0.1

def causal_filter(signal, filter_taps):
    length_now = signal.shape[0]
    padded = jnp.concatenate([jnp.zeros((CONV - 1, signal.shape[1]), jnp.float32), signal], axis=0)
    result = filter_taps[CONV]
    for offset in range(CONV):
        result = result + filter_taps[offset] * padded[offset:offset + length_now]
    return result

def block_step(state_now, inputs):
    values, step_sizes, log_decay, writer, reader = inputs
    cumulative = jnp.cumsum(log_decay, axis=0)
    causal = (jnp.arange(BLOCK)[:, None] >= jnp.arange(BLOCK)[None, :])[:, :, None]
    decay_mask = jnp.exp(jnp.where(causal, cumulative[:, None, :] - cumulative[None, :, :], -jnp.inf))
    scores = jnp.dot(reader, writer.T, precision=highest, preferred_element_type=jnp.float32)
    weights = scores[:, :, None] * decay_mask * step_sizes[None, :, :]
    within = jnp.einsum('tsh,shp->thp', weights, values, precision=highest)
    carried = jnp.einsum('tn,hnp->thp', reader, state_now, precision=highest) * jnp.exp(cumulative)[:, :, None]
    tail_weight = jnp.exp(cumulative[-1][None, :] - cumulative) * step_sizes
    state_next = jnp.exp(cumulative[-1])[:, None, None] * state_now + jnp.einsum('sn,shp->hnp', writer, tail_weight[:, :, None] * values, precision=highest)
    return (state_next, within + carried)

def scan_heads(values, step_sizes, log_decay, writer, reader):
    blocks = values.shape[0] // BLOCK

    def blocked(array):
        return array.reshape((blocks, BLOCK) + array.shape[1:])
    initial = jnp.zeros((values.shape[1], STATE, values.shape[2]), jnp.float32)
    last_state, outputs = lax.scan(jax.checkpoint(block_step), initial, (blocked(values), blocked(step_sizes), blocked(log_decay), blocked(writer), blocked(reader)))
    return outputs.reshape(values.shape)

def mixer_core(main_part, step_raw, state_raw, inner_filter, state_filter, head_params):
    positions = main_part.shape[0]
    heads_here = main_part.shape[1]
    gate_raw = main_part[:, :, :HEAD_DIM]
    signal = main_part[:, :, HEAD_DIM:].reshape(positions, heads_here * HEAD_DIM)
    signal = jax.nn.silu(causal_filter(signal, inner_filter)).reshape(positions, heads_here, HEAD_DIM)
    state_signal = jax.nn.silu(causal_filter(state_raw, state_filter))
    writer = state_signal[:, :STATE]
    reader = state_signal[:, STATE:]
    step_sizes = jax.nn.softplus(step_raw + head_params[0])
    log_decay = -step_sizes * jnp.exp(head_params[1])
    scanned = scan_heads(signal, step_sizes, log_decay, writer, reader) + head_params[2][None, :, None] * signal
    return (scanned * jax.nn.silu(gate_raw)).reshape(positions, heads_here * HEAD_DIM)

def forward(sequence_in, length_now, weights_in):
    inner_weight, step_weight, state_weight, output_weight, inner_filter, state_filter, head_params, norm_gain = weights_in
    main_width = HEADS * 2 * HEAD_DIM
    combined = jnp.concatenate([inner_weight.reshape(D, main_width), step_weight, state_weight], axis=1)
    projected = low_back(jnp.dot(sequence_in, low(combined), precision=highest, preferred_element_type=jnp.float32))
    main_part = projected[:, :main_width].reshape(SEQ_LEN, HEADS, 2 * HEAD_DIM)
    step_raw = projected[:, main_width:main_width + HEADS]
    state_raw = projected[:, main_width + HEADS:]
    gated_out = mixer_core(main_part, step_raw, state_raw, inner_filter, state_filter, head_params)
    norm_scale = lax.rsqrt(lax.optimization_barrier(jnp.mean(gated_out * gated_out, axis=1, keepdims=True)) + eps_norm)
    normed = low(gated_out * norm_scale * norm_gain)
    branch = jnp.dot(normed, low(output_weight).T, precision=highest, preferred_element_type=jnp.float32)
    live_mask = (jnp.arange(SEQ_LEN) < length_now).astype(jnp.float32)
    return sequence_in + live_mask[:, None] * branch

def adam_rows(weight_now, gradient, moments, decayed):
    first_moment = beta_one * moments[0] + (1.0 - beta_one) * gradient
    second_moment = beta_two * moments[1] + (1.0 - beta_two) * gradient * gradient
    direction = first_moment / (1.0 - beta_one ** STEP) / (jnp.sqrt(second_moment / (1.0 - beta_two ** STEP)) + adam_eps)
    if decayed:
        direction = direction + decay_rate * weight_now
    return jnp.stack([first_moment, second_moment, direction])

def reference(tokens, cotangent, lengths, inner_weight, step_weight, state_weight, output_weight, inner_filter, state_filter, head_params, norm_gain, inner_moments, step_moments, state_moments, output_moments, inner_filter_moments, state_filter_moments, head_moments, gain_moments):
    params = (inner_weight, step_weight, state_weight, output_weight, inner_filter, state_filter, head_params, norm_gain)
    sequences_in = tokens.astype(jnp.float32).reshape(SEQS, SEQ_LEN, D)
    cotangent_in = cotangent.astype(jnp.float32).reshape(SEQS, SEQ_LEN, D)

    def per_sequence(totals, inputs):
        sequence_now, cotangent_now, length_now = inputs
        outputs, pullback = jax.vjp(lambda sequence_arg, weights_arg: forward(sequence_arg, length_now, weights_arg), sequence_now, params)
        sequence_grad, weight_grads = pullback(cotangent_now)
        totals = jax.tree.map(lambda total_now, extra: total_now + extra, totals, weight_grads)
        return (totals, (outputs.astype(jnp.bfloat16), sequence_grad.astype(jnp.bfloat16)))
    zero_grads = jax.tree.map(jnp.zeros_like, params)
    grads_all, (mixed, tokens_gradient) = lax.scan(per_sequence, zero_grads, (sequences_in, cotangent_in, lengths))
    moments_all = (inner_moments, step_moments, state_moments, output_moments, inner_filter_moments, state_filter_moments, head_moments, gain_moments)
    decayed_flags = (True, True, True, True, True, True, False, False)
    updates = [adam_rows(weight_now, gradient, moments, flag) for weight_now, gradient, moments, flag in zip(params, grads_all, moments_all, decayed_flags)]
    return (mixed.reshape(TOKENS, D), tokens_gradient.reshape(TOKENS, D), grads_all[0], grads_all[1], grads_all[2], grads_all[3], grads_all[4], grads_all[5], grads_all[6], grads_all[7], updates[0], updates[1], updates[2], updates[3], updates[4], updates[5], updates[6], updates[7])
```

```python
import functools

import jax
import jax.numpy as jnp
from jax import lax
from jax.experimental import pallas as pl
from jax.experimental.pallas import tpu as pltpu
from jax.sharding import PartitionSpec as P

HEAD_DIM = 64
STATE = 128
CONV = 4
BLOCK = 256
STEP = 100
INNER = 4096

highest = lax.Precision.HIGHEST
eps_norm = 1e-05
beta_one = 0.9
beta_two = 0.95
adam_eps = 1e-08
decay_rate = 0.1

f32 = jnp.float32
bf16 = jnp.bfloat16

KINDS = 5
A_COL, EA_COL, W_COL, WDEV_COL, EADEV_COL = range(KINDS)


def dot(left, right, dims=((1,), (0,))):
    return lax.dot_general(left, right, (dims, ((), ())), preferred_element_type=f32)


NT = ((1,), (1,))


def exact_dot(left, right, dims=((1,), (0,))):
    return lax.dot_general(
        left, right, (dims, ((), ())), precision=highest, preferred_element_type=f32
    )


def sigmoid(value):
    return 1.0 / (1.0 + jnp.exp(-value))


def expand(cols, kind, heads):
    rows = cols.shape[0]
    first = lax.broadcasted_iota(jnp.int32, (rows, 128), 1) < HEAD_DIM
    tiles = []
    for pair in range(heads // 2):
        at = kind * heads + 2 * pair
        tiles.append(jnp.where(first, cols[:, at : at + 1], cols[:, at + 1 : at + 2]))
    return tiles[0] if len(tiles) == 1 else jnp.concatenate(tiles, axis=1)


def head_sums(value, heads):
    first = lax.broadcasted_iota(jnp.int32, (value.shape[0], 128), 1) < HEAD_DIM
    sums = []
    for pair in range(heads // 2):
        tile = value[:, 128 * pair : 128 * (pair + 1)]
        sums.append(jnp.sum(jnp.where(first, tile, 0.0), axis=1, keepdims=True))
        sums.append(jnp.sum(jnp.where(first, 0.0, tile), axis=1, keepdims=True))
    return sums


def head_mask(width, head):
    lanes = lax.broadcasted_iota(jnp.int32, (1, width), 1)
    return jnp.where(lanes // HEAD_DIM == head, 1.0, 0.0).astype(bf16)


def block_rows(index):
    return pl.ds(pl.multiple_of(index * BLOCK, BLOCK), BLOCK)


def filtered(extended, taps, base):
    result = taps[CONV : CONV + 1]
    for offset in range(CONV):
        begin = base + 8 - (CONV - 1) + offset
        result = result + taps[offset : offset + 1] * extended[begin : begin + BLOCK]
    return result


def decay_of(cols_block, arow_ref, block, head, heads, causal):
    column = cols_block[:, A_COL * heads + head : A_COL * heads + head + 1]
    row = arow_ref[0, block, head : head + 1, :]
    return jnp.exp(jnp.where(causal, column - row, -jnp.inf))


def causal_mask():
    rows = lax.broadcasted_iota(jnp.int32, (BLOCK, BLOCK), 0)
    return rows >= lax.broadcasted_iota(jnp.int32, (BLOCK, BLOCK), 1)


def load_signal(part_ref, halo_ref, xext, width):
    rows = part_ref.shape[1]
    xext[0:8] = halo_ref[0, :, width:].astype(f32)
    xext[8 : 8 + rows] = part_ref[0, :, width:].astype(f32)


def state_kernel(width, part_ref, halo_ref, par_ref, cols_ref, bt_ref, state_ref, xext, weighted):
    heads = width // HEAD_DIM
    rows = part_ref.shape[1]
    load_signal(part_ref, halo_ref, xext, width)
    taps = par_ref[0, :, width:]
    for block in range(rows // BLOCK):
        at = pl.ds(block * BLOCK, BLOCK)
        u = filtered(xext, taps, block * BLOCK)
        weight = expand(cols_ref[0, at, :], WDEV_COL, heads)
        weighted[at] = (u * sigmoid(u) * weight).astype(bf16)
    state_ref[0] = dot(bt_ref[...], weighted[...])


def forward_kernel(
    width, part_ref, halo_ref, par_ref, cols_ref, arow_ref, b_ref, c_ref, bt_ref, sin_ref,
    gated_ref, sq_ref, xext, signal, scores, state, squares,
):
    heads = width // HEAD_DIM
    rows = part_ref.shape[1]
    blocks = rows // BLOCK

    @pl.when(pl.program_id(0) == 0)
    def _():
        squares[...] = jnp.zeros_like(squares)
        for block in range(blocks):
            at = pl.ds(block * BLOCK, BLOCK)
            scores[block] = exact_dot(c_ref[at], b_ref[at], NT)

    load_signal(part_ref, halo_ref, xext, width)
    taps = par_ref[0, :, width:]
    gain = par_ref[0, 5:6, width:]
    skip = par_ref[0, 6:7, width:]
    for block in range(blocks):
        u = filtered(xext, taps, block * BLOCK)
        signal[pl.ds(block * BLOCK, BLOCK)] = u * sigmoid(u)
    state[...] = sin_ref[0]

    def body(block, carry):
        at = block_rows(block)
        causal = causal_mask()
        cols = cols_ref[0, at, :]
        x = signal[at]
        xl = x.astype(bf16)
        s = state[...].astype(bf16)
        ea = expand(cols, EA_COL, heads)
        y = ea * dot(c_ref[at].astype(bf16), s)
        g = scores[block]
        for head in range(heads):
            m = (g * decay_of(cols, arow_ref, block, head, heads, causal)).astype(bf16)
            y = y + dot(m, xl * head_mask(width, head))
        z = part_ref[0, at, :width].astype(f32)
        gated = (y + skip * x) * (z * sigmoid(z))
        gated_ref[0, at, :] = (gated * gain).astype(bf16)
        sq = gated * gated
        total = sq[:, :128]
        for tile in range(1, width // 128):
            total = total + sq[:, 128 * tile : 128 * (tile + 1)]
        squares[at] += total
        weight = expand(cols, W_COL, heads)
        bt = bt_ref[block]
        state[...] = ea[BLOCK - 1 :] * state[...] + dot(bt, (weight * x).astype(bf16))
        return carry

    lax.fori_loop(0, blocks, body, 0)

    @pl.when(pl.program_id(0) == pl.num_programs(0) - 1)
    def _():
        sq_ref[...] = jnp.sum(squares[...], axis=1, keepdims=True)


def gate_grads(part, normed_grad, gained, par, rowcols, width):
    z = part[:, :width].astype(f32)
    gain = par[5:6, width:]
    gated = gained.astype(f32) * (1.0 / gain)
    grad = rowcols[:, 0:1] * (normed_grad.astype(f32) * gain) - rowcols[:, 1:2] * gated
    sz = sigmoid(z)
    return grad, z * sz, sz * (1.0 + z * (1.0 - sz))


def back_state_kernel(
    width, part_ref, ngrad_ref, gated_ref, par_ref, cols_ref, row_ref, ct_ref,
    dstate_ref, gain_ref, weighted,
):
    heads = width // HEAD_DIM
    rows = part_ref.shape[1]
    gain_sum = jnp.zeros((8, width), f32)
    for block in range(rows // BLOCK):
        at = pl.ds(block * BLOCK, BLOCK)
        ngrad = ngrad_ref[0, at, :]
        gated = gated_ref[0, at, :]
        grad, silu_z, _ = gate_grads(
            part_ref[0, at, :], ngrad, gated, par_ref[0], row_ref[at], width
        )
        weight = expand(cols_ref[0, at, :], EADEV_COL, heads)
        weighted[at] = (grad * silu_z * weight).astype(bf16)
        prod = ngrad.astype(f32) * gated.astype(f32) * row_ref[at, 0:1]
        gain_sum = gain_sum + jnp.sum(prod.reshape(BLOCK // 8, 8, width), axis=0)
    dstate_ref[0] = dot(ct_ref[...], weighted[...])
    gain_ref[0] = gain_sum * (1.0 / par_ref[0, 5:6, width:])


def product_terms(left, right):
    lane = lax.broadcasted_iota(jnp.int32, (left.shape[0], 128), 1)
    first = lane < HEAD_DIM
    terms = []
    for pair in range(left.shape[1] // 128):
        tile = slice(128 * pair, 128 * (pair + 1))
        value = left[:, tile]
        other = right[:, tile]
        value_high = value.astype(bf16).astype(f32)
        other_high = other.astype(bf16).astype(f32)
        value_low = value - value_high
        other_low = (other - other_high).astype(bf16)
        turned_high = pltpu.roll(value_high, HEAD_DIM, 1)
        turned_low = pltpu.roll(value_low, HEAD_DIM, 1)
        other_turned = pltpu.roll(other_high, HEAD_DIM, 1)
        for even in (True, False):
            if even:
                one = jnp.where(first, value_high, turned_low)
                two = jnp.where(first, value_high, 0.0)
                both = jnp.where(first, other_high, other_turned)
            else:
                one = jnp.where(first, turned_high, value_low)
                two = jnp.where(first, 0.0, value_high)
                both = jnp.where(first, other_turned, other_high)
            terms.append(
                (
                    jnp.concatenate([one.astype(bf16), two.astype(bf16)], axis=1),
                    jnp.concatenate([both.astype(bf16), other_low], axis=1),
                )
            )
    return terms


def fold_rows(value):
    return jnp.sum(value.reshape(value.shape[0] // 8, 8, value.shape[1]), axis=0)


def backward_kernel(
    width, part_ref, halo_ref, ngrad_ref, gated_ref, par_ref, cols_ref, arow_ref, row_ref,
    b_ref, c_ref, bt_ref, ct_ref, sin_ref, din_ref,
    dpart_ref, tail_ref, head_ref, sums_ref, dcols_ref, dbc_ref,
    xext, uval, scores, dscores, states, dstate, duext, skip_sum, dbacc, dcacc,
):
    heads = width // HEAD_DIM
    rows = part_ref.shape[1]
    blocks = rows // BLOCK
    step = pl.program_id(0)

    @pl.when(step == 0)
    def _():
        dscores[...] = jnp.zeros_like(dscores)
        dbacc[...] = jnp.zeros_like(dbacc)
        dcacc[...] = jnp.zeros_like(dcacc)
        for block in range(blocks):
            at = pl.ds(block * BLOCK, BLOCK)
            scores[block] = exact_dot(c_ref[at], b_ref[at], NT)

    load_signal(part_ref, halo_ref, xext, width)
    taps = par_ref[0, :, width:]
    skip = par_ref[0, 6:7, width:]
    for block in range(blocks):
        uval[pl.ds(block * BLOCK, BLOCK)] = filtered(xext, taps, block * BLOCK)
    states[0] = sin_ref[0]
    dstate[...] = din_ref[0]
    skip_sum[...] = jnp.zeros_like(skip_sum)

    def state_body(block, carry):
        at = block_rows(block)
        cols = cols_ref[0, at, :]
        u = uval[at]
        weight = expand(cols, W_COL, heads)
        last = expand(cols[BLOCK - 8 :], EA_COL, heads)[7:8]
        states[block + 1] = last * states[block] + dot(
            bt_ref[block], (weight * (u * sigmoid(u))).astype(bf16)
        )
        return carry

    lax.fori_loop(0, blocks, state_body, 0)

    def body(count, carry):
        block = blocks - 1 - count
        at = block_rows(block)
        causal = causal_mask()
        cols = cols_ref[0, at, :]
        part = part_ref[0, at, :]
        grad, silu_z, slope_z = gate_grads(
            part, ngrad_ref[0, at, :], gated_ref[0, at, :], par_ref[0], row_ref[at], width
        )
        u = uval[at]
        su = sigmoid(u)
        x = u * su
        xl = x.astype(bf16)
        dy = grad * silu_z
        dyl = dy.astype(bf16)
        dyt = dy.T.astype(bf16)
        s = states[block].astype(bf16)
        d = dstate[...]
        dl = d.astype(bf16)
        ea = expand(cols, EA_COL, heads)
        weight = expand(cols, W_COL, heads)
        b = b_ref[at].astype(bf16)
        c = c_ref[at].astype(bf16)
        g = scores[block]
        y = ea * dot(c, s)
        dg = dscores[block]
        terms = product_terms(dy, x)
        dxt = []
        for head in range(heads):
            decay = decay_of(cols, arow_ref, block, head, heads, causal)
            m = (g * decay).astype(bf16)
            keep = head_mask(width, head)
            y = y + dot(m, xl * keep)
            dm = dot(terms[head][0], terms[head][1], NT)
            dg = dg + dm * decay
            dxt.append(dot(dyt[HEAD_DIM * head : HEAD_DIM * (head + 1)], m))
        dscores[block] = dg
        dx = jnp.concatenate(dxt, axis=0).T + weight * dot(b, dl)
        xf = xl.astype(f32)
        zz = xf * dx
        da = dyl.astype(f32) * y - zz
        ends = jnp.sum(states[block + 1] * d, axis=0, keepdims=True)
        is_last = lax.broadcasted_iota(jnp.int32, (BLOCK, 1), 0) == BLOCK - 1
        da = da + jnp.where(is_last, ends, 0.0)
        columns = head_sums(da, heads) + head_sums(zz, heads)
        lanes = lax.broadcasted_iota(jnp.int32, (BLOCK, 2 * heads), 1)
        packed = jnp.broadcast_to(columns[0], (BLOCK, 2 * heads))
        for at_lane in range(1, 2 * heads):
            packed = jnp.where(lanes == at_lane, columns[at_lane], packed)
        dcols_ref[0, at, :] = packed
        edy = (ea * dy).astype(bf16)
        dcacc[at] += dot(edy, s, NT)
        dbacc[at] += dot((weight * x).astype(bf16), dl, NT)
        dstate[...] = ea[BLOCK - 1 :] * d + dot(ct_ref[block], edy)
        du = (dx + skip * dy) * (su * (1.0 + u * (1.0 - su)))
        duext[at] = du
        skip_sum[...] += fold_rows(dy * x)
        dz = grad * (y + skip * x) * slope_z
        dpart_ref[0, at, :width] = dz.astype(bf16)
        return carry

    lax.fori_loop(0, blocks, body, 0)
    duext[rows : rows + 8] = jnp.zeros((8, width), f32)

    tap_sums = [jnp.zeros((8, width), f32) for _ in range(CONV + 1)]
    for block in range(blocks):
        base = block * BLOCK
        du = duext[base : base + BLOCK]
        dx = taps[CONV - 1 : CONV] * du
        tap_sums[CONV] = tap_sums[CONV] + fold_rows(du)
        for offset in range(CONV):
            begin = base + 8 - (CONV - 1) + offset
            tap_sums[offset] = tap_sums[offset] + fold_rows(du * xext[begin : begin + BLOCK])
            if offset < CONV - 1:
                ahead = base + CONV - 1 - offset
                dx = dx + taps[offset : offset + 1] * duext[ahead : ahead + BLOCK]
        dpart_ref[0, base : base + BLOCK, width:] = dx.astype(bf16)
        if block == blocks - 1:
            tail_ref[0, :, width:] = dx[BLOCK - 16 :]
    tail_ref[0, :, :width] = dpart_ref[0, rows - 16 : rows, :width].astype(f32)
    head_ref[0, :, :width] = jnp.zeros((8, width), f32)
    head_ref[0, :, width:] = duext[0:8]
    lines = tap_sums + [jnp.zeros((8, width), f32), skip_sum[...]]
    out_rows = [jnp.sum(line, axis=0, keepdims=True) for line in lines]
    sums_ref[0] = jnp.concatenate(out_rows + [jnp.zeros((1, width), f32)], axis=0)

    @pl.when(step == pl.num_programs(0) - 1)
    def _():
        for block in range(blocks):
            at = pl.ds(block * BLOCK, BLOCK)
            dg = dscores[block]
            dbc_ref[at, :STATE] = dbacc[at] + exact_dot(dg.T, c_ref[at])
            dbc_ref[at, STATE:] = dcacc[at] + exact_dot(dg, b_ref[at])


def run_kernels(rows, shards, width):
    heads = width // HEAD_DIM
    steps = shards
    blocks = rows // BLOCK
    chans = width

    def over(rows_here, lanes):
        return pl.BlockSpec((1, rows_here, lanes), lambda i: (i, 0, 0))

    def each(*dims):
        return pl.BlockSpec((1,) + dims, lambda i: (i,) + (0,) * len(dims))

    def whole(*dims):
        return pl.BlockSpec(dims, lambda i: (0,) * len(dims))

    part = over(rows, 2 * width)
    halo = over(8, 2 * width)
    par = over(8, 2 * width)
    chan = over(rows, width)
    cols = each(rows, KINDS * heads)
    arow = each(blocks, heads, BLOCK)
    state = over(STATE, width)
    bc = whole(rows, STATE)
    bct = whole(blocks, STATE, BLOCK)
    bct_flat = whole(STATE, rows)
    rowcols = whole(rows, 2)
    shape = jax.ShapeDtypeStruct
    params = pltpu.CompilerParams(
        dimension_semantics=("arbitrary",), vmem_limit_bytes=56 * 1024 * 1024
    )
    elements = rows * shards * chans

    def cost(per_element, reads):
        return pl.CostEstimate(
            flops=elements * per_element, bytes_accessed=elements * reads, transcendentals=0
        )

    local_state = pl.pallas_call(
        functools.partial(state_kernel, width),
        grid=(steps,),
        in_specs=[part, halo, par, cols, bct_flat],
        out_specs=state,
        out_shape=shape((shards, STATE, chans), f32),
        scratch_shapes=[pltpu.VMEM((rows + 8, width), f32), pltpu.VMEM((rows, width), bf16)],
        compiler_params=params,
        cost_estimate=cost(7000, 8),
        name="local_state",
    )
    forward = pl.pallas_call(
        functools.partial(forward_kernel, width),
        grid=(steps,),
        in_specs=[part, halo, par, cols, arow, bc, bc, bct, state],
        out_specs=[chan, whole(rows, 1)],
        out_shape=[shape((shards, rows, chans), bf16), shape((rows, 1), f32)],
        scratch_shapes=[
            pltpu.VMEM((rows + 8, width), f32),
            pltpu.VMEM((rows, width), f32),
            pltpu.VMEM((blocks, BLOCK, BLOCK), f32),
            pltpu.VMEM((STATE, width), f32),
            pltpu.VMEM((rows, 128), f32),
        ],
        compiler_params=params,
        cost_estimate=cost(17000, 10),
        name="forward_scan",
    )
    back_state = pl.pallas_call(
        functools.partial(back_state_kernel, width),
        grid=(steps,),
        in_specs=[part, chan, chan, par, cols, rowcols, bct_flat],
        out_specs=[state, over(8, width)],
        out_shape=[shape((shards, STATE, chans), f32), shape((shards, 8, chans), f32)],
        scratch_shapes=[pltpu.VMEM((rows, width), bf16)],
        compiler_params=params,
        cost_estimate=cost(8000, 14),
        name="back_state",
    )
    backward = pl.pallas_call(
        functools.partial(backward_kernel, width),
        grid=(steps,),
        in_specs=[
            part, halo, chan, chan, par, cols, arow, rowcols, bc, bc, bct, bct, state, state
        ],
        out_specs=[
            part, over(16, 2 * width), over(8, 2 * width), over(8, width),
            each(rows, 2 * heads), whole(rows, 2 * STATE),
        ],
        out_shape=[
            shape((shards, rows, 2 * chans), bf16),
            shape((shards, 16, 2 * chans), f32),
            shape((shards, 8, 2 * chans), f32),
            shape((shards, 8, chans), f32),
            shape((steps, rows, 2 * heads), f32),
            shape((rows, 2 * STATE), f32),
        ],
        scratch_shapes=[
            pltpu.VMEM((rows + 8, width), f32),
            pltpu.VMEM((rows, width), f32),
            pltpu.VMEM((blocks, BLOCK, BLOCK), f32),
            pltpu.VMEM((blocks, BLOCK, BLOCK), f32),
            pltpu.VMEM((blocks + 1, STATE, width), f32),
            pltpu.VMEM((STATE, width), f32),
            pltpu.VMEM((rows + 8, width), f32),
            pltpu.VMEM((8, width), f32),
            pltpu.VMEM((rows, STATE), f32),
            pltpu.VMEM((rows, STATE), f32),
        ],
        compiler_params=params,
        cost_estimate=cost(43000, 20),
        name="backward_scan",
    )
    return local_state, forward, back_state, backward


def after(value, *others):
    def body(*refs):
        del refs

    anywhere = pl.BlockSpec(memory_space=pl.ANY)
    return pl.pallas_call(
        body,
        in_specs=[anywhere] * (1 + len(others)),
        out_specs=anywhere,
        out_shape=jax.ShapeDtypeStruct(value.shape, value.dtype),
        input_output_aliases={0: 0},
        name="after",
    )(value, *others)


def dp_sum(array):
    size = lax.axis_size("dp")
    total = array
    for k in range(1, size):
        total = total + lax.ppermute(array, "dp", [(i, (i + k) % size) for i in range(size)])
    return total


def dp_gather(array, *meanwhile):
    size = lax.axis_size("dp")
    me = lax.axis_index("dp")
    rows = array.shape[0]
    full = jnp.zeros((size * rows,) + array.shape[1:], array.dtype)
    full = lax.dynamic_update_slice(full, array, (me * rows, 0))
    for k in range(1, size):
        got = lax.ppermute(array, "dp", [(i, (i + k) % size) for i in range(size)])
        if meanwhile:
            got = after(got, *meanwhile)
        full = lax.dynamic_update_slice(full, got, (lax.rem(me - k + size, size) * rows, 0))
    return full


def dp_scatter(array, *meanwhile):
    size = lax.axis_size("dp")
    me = lax.axis_index("dp")
    part = array.shape[-1] // size
    total = lax.dynamic_slice_in_dim(array, me * part, part, array.ndim - 1).astype(f32)
    for k in range(1, size):
        there = lax.rem(me + k, size)
        piece = lax.dynamic_slice_in_dim(array, there * part, part, array.ndim - 1)
        got = lax.ppermute(piece, "dp", [(i, (i + k) % size) for i in range(size)])
        if meanwhile:
            got = after(got, *meanwhile)
        total = total + got.astype(f32)
    return total


def carried_states(own, totals, reverse):
    devices = lax.axis_size("mp")
    me = lax.axis_index("mp")
    shards, _, chans = own.shape

    def over_channels(logs):
        per_chan = jnp.repeat(logs.reshape(shards, 1, -1), HEAD_DIM, axis=-1)
        return jnp.exp(per_chan)

    result = jnp.zeros_like(own)
    result_log = jnp.zeros_like(totals[0])
    group_logs = totals
    span = 1
    while span < devices:
        got = lax.ppermute(own.astype(bf16), "mp", [(i, i ^ span) for i in range(devices)])
        got = got.astype(f32)
        high = lax.rem(me // span, 2) == 1
        nearer = jnp.logical_not(high) if reverse else high
        mine_log = lax.dynamic_index_in_dim(group_logs, me // span, 0, keepdims=False)
        theirs = lax.bitwise_xor(me // span, 1)
        their_log = lax.dynamic_index_in_dim(group_logs, theirs, 0, keepdims=False)
        result = result + jnp.where(nearer, over_channels(result_log), 0.0) * got
        result_log = result_log + jnp.where(nearer, their_log, 0.0)
        if 2 * span < devices:
            own = jnp.where(nearer, 1.0, over_channels(their_log)) * own
            own = own + jnp.where(nearer, over_channels(mine_log), 1.0) * got
        group_logs = group_logs.reshape(-1, 2, totals.shape[1]).sum(axis=1)
        span *= 2
    return result


def causal_filter(extended, taps, rows):
    result = taps[CONV]
    for offset in range(CONV):
        begin = 8 - (CONV - 1) + offset
        result = result + taps[offset] * extended[begin : begin + rows]
    return result


def adam_rows(weight_now, gradient, moments, decayed):
    first_moment = beta_one * moments[0] + (1.0 - beta_one) * gradient
    second_moment = beta_two * moments[1] + (1.0 - beta_two) * gradient * gradient
    direction = (
        first_moment
        / (1.0 - beta_one**STEP)
        / (jnp.sqrt(second_moment / (1.0 - beta_two**STEP)) + adam_eps)
    )
    if decayed:
        direction = direction + decay_rate * weight_now
    return jnp.stack([first_moment, second_moment, direction])


def local(
    tokens,
    cotangent,
    lengths,
    inner_weight,
    step_weight,
    state_weight,
    output_weight,
    inner_filter,
    state_filter,
    head_params,
    norm_gain,
    inner_moments,
    step_moments,
    state_moments,
    output_moments,
    inner_filter_moments,
    state_filter_moments,
    head_moments,
    gain_moments,
):
    shards = lax.axis_size("mp")
    mine = lax.axis_index("mp")
    rows, model = tokens.shape
    own_model, heads_here, _ = inner_weight.shape
    chans = heads_here * HEAD_DIM
    width = min(256, chans)
    step_heads = width // HEAD_DIM
    groups = chans // width
    heads = shards * heads_here
    blocks = rows // BLOCK
    onward = [(i, i + 1) for i in range(shards - 1)]
    homeward = [(i + 1, i) for i in range(shards - 1)]
    local_state, forward, back_state, backward = run_kernels(rows, shards, width)

    inner_groups = inner_weight.reshape(own_model, groups, step_heads, 2, HEAD_DIM)
    inner_groups = inner_groups.astype(bf16).transpose(1, 0, 3, 2, 4)
    inner_groups = inner_groups.reshape(groups, own_model, 2 * width)
    out_groups = output_weight.astype(bf16).reshape(own_model, groups, width)

    packed = jnp.concatenate(
        [
            inner_filter,
            norm_gain[None],
            jnp.repeat(head_params[2], HEAD_DIM)[None],
            jnp.pad(head_params[:2].reshape(1, -1), ((0, 0), (0, chans - 2 * heads_here))),
        ],
        axis=0,
    )
    own_lines = packed.shape[0]
    packed = jnp.concatenate([packed, step_weight.reshape(-1, chans)], axis=0)
    packed = lax.all_gather(packed, "mp", axis=0)
    head_rows = packed[:, 7, : 2 * heads_here].reshape(shards, 2, heads_here)
    step_bias = head_rows[:, 0].reshape(heads)
    decay_base = jnp.exp(head_rows[:, 1].reshape(heads))
    step_all = packed[:, own_lines:].reshape(shards, own_model, heads_here)
    step_all = step_all.astype(bf16).transpose(1, 0, 2).reshape(own_model, heads)
    packed = packed[:, :own_lines]
    params = []
    for group in range(groups):
        here = packed[:, :, group * width : (group + 1) * width]
        params.append(jnp.concatenate([jnp.zeros_like(here), here], axis=-1))

    small_own = jnp.concatenate([step_all, state_weight.astype(bf16)], axis=1)
    inner_low = [dp_gather(inner_groups[0])]
    small = dp_gather(after(small_own, inner_low[0]))

    raw_small = jnp.dot(tokens, small, preferred_element_type=f32)
    state_raw = raw_small[:, heads:]
    state_halo = lax.ppermute(state_raw[rows - 8 :], "mp", onward)
    state_ext = jnp.concatenate([state_halo, state_raw], axis=0)
    state_u = causal_filter(state_ext, state_filter, rows)
    state_sig = jax.nn.sigmoid(state_u)
    state_signal = state_u * state_sig
    writer = state_signal[:, :STATE]
    reader = state_signal[:, STATE:]
    writer_t = writer.T.astype(bf16)
    reader_t = reader.T.astype(bf16)
    writer_blocks = writer_t.reshape(STATE, blocks, BLOCK).transpose(1, 0, 2)
    reader_blocks = reader_t.reshape(STATE, blocks, BLOCK).transpose(1, 0, 2)
    step_arg = raw_small[:, :heads] + step_bias
    step_sizes = jax.nn.softplus(step_arg)
    log_decay = -step_sizes * decay_base
    lower = (jnp.arange(BLOCK)[:, None] >= jnp.arange(BLOCK)[None, :]).astype(f32)
    cumulative = jnp.einsum(
        "ts,bsh->bth", lower, log_decay.reshape(blocks, BLOCK, heads), precision=highest
    )
    block_total = cumulative[:, -1]
    running = jnp.cumsum(block_total, axis=0)
    before = running - block_total
    device_total = running[-1]
    dt_blocks = step_sizes.reshape(blocks, BLOCK, heads)
    from_start = cumulative + before[:, None]
    kinds = [
        cumulative,
        jnp.exp(cumulative),
        jnp.exp(block_total[:, None] - cumulative) * dt_blocks,
        jnp.exp(device_total - from_start) * dt_blocks,
        jnp.exp(from_start),
    ]
    by_group = (shards, groups, step_heads)
    columns = jnp.stack(kinds).reshape((KINDS, rows) + by_group)
    columns = [
        columns[:, :, :, group].transpose(2, 1, 0, 3).reshape(shards, rows, KINDS * step_heads)
        for group in range(groups)
    ]
    arows = (cumulative - jnp.log(dt_blocks)).reshape((blocks, BLOCK) + by_group)
    arows = arows.transpose(3, 2, 0, 4, 1)

    totals_all = lax.all_gather(device_total, "mp", axis=0)
    totals_groups = totals_all.reshape((shards,) + by_group).transpose(2, 0, 1, 3)
    totals_groups = totals_groups.reshape(groups, shards, shards * step_heads)

    for group in range(1, groups):
        inner_low.append(dp_gather(after(inner_groups[group], small), columns[0], totals_all))
    inner_full = [lax.all_gather(own, "mp", axis=0) for own in inner_low]
    parts, halos, states_in, gained = [], [], [], []
    squares = 0.0
    ready = [columns[0]]
    for group in range(groups):
        inner_full[group] = after(inner_full[group], *ready)
        part = jnp.einsum(
            "td,mdc->mtc", tokens, inner_full[group], preferred_element_type=f32
        )
        halo = lax.ppermute(part[:, rows - 8 :], "mp", onward)
        if group == 0:
            out_low = [
                dp_gather(after(out_groups[:, g], inner_low[-1]), halo) for g in range(groups)
            ]
            out_full = [lax.all_gather(own, "mp", axis=0) for own in out_low]
            halo = after(halo, *out_low)
        ends = local_state(part, halo, params[group], columns[group], writer_t)
        state_in = carried_states(ends, totals_groups[group], False)
        out, sq = forward(
            part, halo, params[group], columns[group], arows[group], writer, reader,
            writer_blocks, state_in,
        )
        squares = squares + sq
        ready = [out]
        parts.append(part)
        halos.append(halo)
        states_in.append(state_in)
        gained.append(out)
    norm_scale = lax.rsqrt(squares / INNER + eps_norm)
    branch = norm_scale * sum(
        jnp.einsum("mtc,mdc->td", gained[group], out_full[group], preferred_element_type=f32)
        for group in range(groups)
    )
    positions = mine * rows + jnp.arange(rows)
    live = (positions < lengths[0]).astype(f32)[:, None]
    mixed = (tokens.astype(f32) + live * branch).astype(bf16)

    masked = (cotangent.astype(f32) * live).astype(bf16)
    scaled_sum = jnp.sum(masked.astype(f32) * branch, axis=1, keepdims=True)
    row_columns = jnp.concatenate(
        [norm_scale, norm_scale * norm_scale * scaled_sum / INNER], axis=1
    )
    scaled_cot = after((masked.astype(f32) * norm_scale).astype(bf16), row_columns)
    out_parts = [
        jnp.einsum(
            "td,mtc->mcd", scaled_cot, gained[group], preferred_element_type=f32
        ).astype(bf16)
        for group in range(groups)
    ]
    out_sums = [lax.psum_scatter(part, "mp", scatter_dimension=0) for part in out_parts]
    ngrads, starts, gain_sums = [], [], []
    for group in range(groups):
        normed_grad = jnp.einsum(
            "td,mdc->mtc", masked, out_full[group], preferred_element_type=f32
        )
        start, gain_sum = back_state(
            parts[group], normed_grad, gained[group], params[group], columns[group],
            row_columns, reader_t,
        )
        ngrads.append(normed_grad)
        starts.append(start)
        gain_sums.append(gain_sum)
    dstates = [carried_states(starts[g], totals_groups[g], True) for g in range(groups)]
    waiting = out_parts + starts[1:]
    dparts, inner_sums, dbc, all_sums, all_dcols = [], [], 0.0, [], []
    for group in range(groups):
        last = group == groups - 1
        dpart, tail, du_head, sums, dcols, dbc_here = backward(
            parts[group], halos[group], ngrads[group], gained[group], params[group],
            columns[group], arows[group], row_columns, writer, reader, writer_blocks,
            reader_blocks, states_in[group], after(dstates[group], *waiting),
        )
        du_next = lax.ppermute(du_head, "mp", homeward)
        extra = [
            sum(params[group][:, k] * du_next[:, i - k] for k in range(i + 1))
            for i in range(CONV - 1)
        ]
        extra = jnp.concatenate(
            [jnp.zeros((shards, 13, 2 * width), f32), jnp.stack(extra, axis=1)], axis=1
        )
        dpart = lax.dynamic_update_slice(
            dpart, (tail + extra).astype(bf16), (0, rows - 16, 0)
        )
        if last:
            dpart = after(dpart, *inner_sums)
        inner_part = jnp.einsum("td,mtc->mcd", tokens, dpart, preferred_element_type=f32)
        inner_part = inner_part.astype(bf16)
        inner_sums.append(lax.psum_scatter(inner_part, "mp", scatter_dimension=0))
        waiting = [inner_part] + (out_sums if group == groups - 2 else [])
        dparts.append(dpart)
        dbc = dbc + dbc_here
        all_sums.append(sums)
        all_dcols.append(dcols)
    dbc = after(dbc, inner_part)
    all_dcols[-1] = after(all_dcols[-1], inner_part)

    dcols = jnp.stack(all_dcols).reshape(groups, shards, rows, 2, step_heads)
    dcols = dcols.transpose(3, 2, 1, 0, 4).reshape(2, rows, heads)
    dlog = jnp.einsum(
        "st,bsh->bth", lower, dcols[0].reshape(blocks, BLOCK, heads), precision=highest
    ).reshape(rows, heads)
    slope = jax.nn.sigmoid(step_arg)
    ratio = jnp.where(step_sizes > 1e-20, slope / jnp.maximum(step_sizes, 1e-20), 1.0)
    dstep = dcols[1] * ratio - dlog * decay_base * slope
    sums = jnp.concatenate(all_sums, axis=-1)
    gains = jnp.concatenate(gain_sums, axis=-1)
    head_line = jnp.concatenate(
        [
            jnp.sum(dstep, axis=0).reshape(shards, heads_here),
            jnp.sum(dlog * log_decay, axis=0).reshape(shards, heads_here),
            jnp.sum(sums[:, 6].reshape(shards, heads_here, HEAD_DIM), axis=-1),
        ],
        axis=1,
    )
    head_line = jnp.pad(head_line, ((0, 0), (0, chans - 3 * heads_here)))[:, None]
    du_state = dbc * (state_sig * (1.0 + state_u * (1.0 - state_sig)))
    du_state_next = lax.ppermute(du_state[:8], "mp", homeward)
    du_state_ext = jnp.concatenate([du_state, du_state_next], axis=0)
    dstate_raw = sum(
        state_filter[k] * du_state_ext[CONV - 1 - k : CONV - 1 - k + rows] for k in range(CONV)
    )
    state_filter_part = jnp.stack(
        [jnp.sum(du_state * state_ext[5 + k : 5 + k + rows], axis=0) for k in range(CONV)]
        + [jnp.sum(du_state, axis=0)]
    )
    dsmall = jnp.concatenate([dstep, dstate_raw], axis=1).astype(bf16)

    small_grad = lax.dot_general(
        dsmall, tokens, (((0,), (0,)), ((), ())), preferred_element_type=f32
    )
    state_share = 2 * STATE // shards
    lines = -(-(CONV + 1) * 2 * STATE // chans)
    filter_lines = jnp.pad(
        state_filter_part.reshape(-1), (0, lines * chans - (CONV + 1) * 2 * STATE)
    )
    filter_lines = jnp.broadcast_to(filter_lines.reshape(1, lines, chans), (shards, lines, chans))
    sums_here = jnp.concatenate(
        [sums[:, : CONV + 1], jnp.sum(gains, axis=1, keepdims=True), head_line, filter_lines],
        axis=1,
    ).reshape(shards, -1)
    sum_rows = -(-sums_here.shape[1] // model)
    sum_size = sums_here.shape[1]
    sums_here = jnp.pad(sums_here, ((0, 0), (0, sum_rows * model - sum_size)))
    small_grad = jnp.concatenate(
        [
            small_grad[:heads].reshape(shards, heads_here, model),
            small_grad[heads:].reshape(shards, state_share, model),
            sums_here.reshape(shards, sum_rows, model),
        ],
        axis=1,
    )
    small_rows = heads_here + state_share
    small_total = lax.psum_scatter(after(small_grad, inner_sums[-1]), "mp", scatter_dimension=0)

    input_part = 0.0
    for group in range(groups):
        input_part = input_part + jnp.einsum(
            "mtc,mdc->td", after(dparts[group], small_grad), inner_full[group], preferred_element_type=f32,
        )
    small_part = lax.dot_general(dsmall, small, (NT, ((), ())), preferred_element_type=f32)
    tokens_gradient = (cotangent.astype(f32) + input_part + small_part).astype(bf16)

    early = [after(total, inner_part) for total in out_sums + inner_sums[:-1]]
    early = [dp_scatter(total, tokens_gradient) for total in early]
    out_grads, inner_grads = early[:groups], early[groups:]
    inner_grads.append(dp_scatter(inner_sums[-1]))
    small_sum = dp_scatter(small_total[:small_rows])
    own = dp_sum(small_total[small_rows:]).reshape(-1)[:sum_size].reshape(-1, chans)
    step_gradient = small_sum[:heads_here].T
    state_gradient = lax.all_gather(small_sum[heads_here:], "mp", axis=0, tiled=True).T
    output_gradient = jnp.concatenate(out_grads, axis=0).T
    inner_gradient = jnp.stack(inner_grads)
    inner_gradient = inner_gradient.reshape(groups, 2, step_heads, HEAD_DIM, own_model)
    inner_gradient = inner_gradient.transpose(4, 0, 2, 1, 3)
    inner_gradient = inner_gradient.reshape(own_model, heads_here, 2 * HEAD_DIM)
    state_filter_gradient = own[CONV + 3 :].reshape(-1)[: (CONV + 1) * 2 * STATE]
    state_filter_gradient = state_filter_gradient.reshape(CONV + 1, 2 * STATE)
    inner_filter_gradient = own[: CONV + 1]
    gain_gradient = own[CONV + 1]
    head_gradient = own[CONV + 2, : 3 * heads_here].reshape(3, heads_here)

    inner_update = adam_rows(inner_weight, inner_gradient, inner_moments, True)
    step_update = adam_rows(step_weight, step_gradient, step_moments, True)
    state_update = adam_rows(state_weight, state_gradient, state_moments, True)
    output_update = adam_rows(output_weight, output_gradient, output_moments, True)
    inner_filter_update = adam_rows(inner_filter, inner_filter_gradient, inner_filter_moments, True)
    state_filter_update = adam_rows(state_filter, state_filter_gradient, state_filter_moments, True)
    head_update = adam_rows(head_params, head_gradient, head_moments, False)
    gain_update = adam_rows(norm_gain, gain_gradient, gain_moments, False)
    return (
        mixed,
        tokens_gradient,
        inner_gradient,
        step_gradient,
        state_gradient,
        output_gradient,
        inner_filter_gradient,
        state_filter_gradient,
        head_gradient,
        gain_gradient,
        inner_update,
        step_update,
        state_update,
        output_update,
        inner_filter_update,
        state_filter_update,
        head_update,
        gain_update,
    )


def solution(mesh):
    return jax.shard_map(
        local,
        mesh=mesh,
        in_specs=(
            P(("dp", "mp"), None),
            P(("dp", "mp"), None),
            P("dp"),
            P("dp", "mp", None),
            P("dp", "mp"),
            P("dp", None),
            P("dp", "mp"),
            P(None, "mp"),
            P(),
            P(None, "mp"),
            P("mp"),
            P(None, "dp", "mp", None),
            P(None, "dp", "mp"),
            P(None, "dp", None),
            P(None, "dp", "mp"),
            P(None, None, "mp"),
            P(),
            P(None, None, "mp"),
            P(None, "mp"),
        ),
        out_specs=(
            P(("dp", "mp"), None),
            P(("dp", "mp"), None),
            P("dp", "mp", None),
            P("dp", "mp"),
            P("dp", None),
            P("dp", "mp"),
            P(None, "mp"),
            P(),
            P(None, "mp"),
            P("mp"),
            P(None, "dp", "mp", None),
            P(None, "dp", "mp"),
            P(None, "dp", None),
            P(None, "dp", "mp"),
            P(None, None, "mp"),
            P(),
            P(None, None, "mp"),
            P(None, "mp"),
        ),
        check_vma=False,
    )
```

```python
import functools

import jax
import jax.numpy as jnp
from jax import lax
from jax.experimental import pallas as pl
from jax.experimental.pallas import tpu as pltpu
from jax.sharding import PartitionSpec as P

HEAD_DIM = 64
STATE = 128
CONV = 4
BLOCK = 256
STEP = 100
INNER = 4096

highest = lax.Precision.HIGHEST
eps_norm = 1e-05
beta_one = 0.9
beta_two = 0.95
adam_eps = 1e-08
decay_rate = 0.1

f32 = jnp.float32
bf16 = jnp.bfloat16

KINDS = 5
A_COL, EA_COL, W_COL, WDEV_COL, EADEV_COL = range(KINDS)


def dot(left, right, dims=((1,), (0,))):
    return lax.dot_general(left, right, (dims, ((), ())), preferred_element_type=f32)


NT = ((1,), (1,))


def exact_dot(left, right, dims=((1,), (0,))):
    return lax.dot_general(
        left, right, (dims, ((), ())), precision=highest, preferred_element_type=f32
    )


def sigmoid(value):
    return 1.0 / (1.0 + jnp.exp(-value))


def expand(cols, kind, heads):
    rows = cols.shape[0]
    first = lax.broadcasted_iota(jnp.int32, (rows, 128), 1) < HEAD_DIM
    tiles = []
    for pair in range(heads // 2):
        at = kind * heads + 2 * pair
        tiles.append(jnp.where(first, cols[:, at : at + 1], cols[:, at + 1 : at + 2]))
    return tiles[0] if len(tiles) == 1 else jnp.concatenate(tiles, axis=1)


def head_sums(one, two, heads):
    width = one.shape[1]
    lanes = lax.broadcasted_iota(jnp.int32, (width, 2 * heads), 0) // HEAD_DIM
    places = lax.broadcasted_iota(jnp.int32, (width, 2 * heads), 1)
    pick_one = jnp.where(lanes == places, 1.0, 0.0).astype(bf16)
    pick_two = jnp.where(lanes + heads == places, 1.0, 0.0).astype(bf16)
    one_high = one.astype(bf16)
    two_high = two.astype(bf16)
    one_low = (one - one_high.astype(f32)).astype(bf16)
    two_low = (two - two_high.astype(f32)).astype(bf16)
    return (dot(one_high, pick_one) + dot(one_low, pick_one)) + (
        dot(two_high, pick_two) + dot(two_low, pick_two)
    )


def head_mask(width, head):
    lanes = lax.broadcasted_iota(jnp.int32, (1, width), 1)
    return jnp.where(lanes // HEAD_DIM == head, 1.0, 0.0).astype(bf16)


def block_rows(index):
    return pl.ds(index * BLOCK, BLOCK)


def filtered(extended, taps, base):
    result = taps[CONV : CONV + 1]
    for offset in range(CONV):
        begin = base + 8 - (CONV - 1) + offset
        result = result + taps[offset : offset + 1] * extended[begin : begin + BLOCK]
    return result


def decay_of(cols_block, arow_ref, block, head, heads, causal):
    column = cols_block[:, A_COL * heads + head : A_COL * heads + head + 1]
    row = arow_ref[0, block, head : head + 1, :]
    return jnp.exp(jnp.where(causal, column - row, -jnp.inf))


def causal_mask():
    rows = lax.broadcasted_iota(jnp.int32, (BLOCK, BLOCK), 0)
    return rows >= lax.broadcasted_iota(jnp.int32, (BLOCK, BLOCK), 1)


def state_kernel(
    width, x_ref, halo_ref, par_ref, cols_ref, bt_ref, state_ref, u_ref, xext, weighted
):
    heads = width // HEAD_DIM
    rows = x_ref.shape[1]
    xext[0:8] = halo_ref[0, :, width:]
    xext[8 : 8 + rows] = x_ref[0]
    taps = par_ref[0, :, width:]
    for block in range(rows // BLOCK):
        at = pl.ds(block * BLOCK, BLOCK)
        u = filtered(xext, taps, block * BLOCK)
        u_ref[0, at, :] = u
        weight = expand(cols_ref[0, at, :], WDEV_COL, heads)
        weighted[at] = (u * sigmoid(u) * weight).astype(bf16)
    state_ref[0] = dot(bt_ref[...], weighted[...])


def forward_kernel(
    width, z_ref, u_ref, par_ref, cols_ref, arow_ref, b_ref, c_ref, bt_ref, sin_ref, *rest
):
    gained_ref, sq_ref, states_ref, scores, squares = rest[-5:]
    heads = width // HEAD_DIM
    rows = z_ref.shape[1]
    blocks = rows // BLOCK

    @pl.when(pl.program_id(0) == 0)
    def _():
        squares[...] = jnp.zeros_like(squares)
        for block in range(blocks):
            at = block_rows(block)
            scores[block] = exact_dot(c_ref[at], b_ref[at], NT)

    gain = par_ref[0, 5:6, width:]
    skip = par_ref[0, 6:7, width:]
    causal = causal_mask()
    state = sin_ref[0]
    states_ref[0, 0] = state
    for block in range(blocks):
        at = block_rows(block)
        cols = cols_ref[0, at, :]
        u = u_ref[0, at, :]
        x = u * sigmoid(u)
        xl = x.astype(bf16)
        ea = expand(cols, EA_COL, heads)
        y = ea * dot(c_ref[at].astype(bf16), state.astype(bf16))
        g = scores[block]
        for head in range(heads):
            m = (g * decay_of(cols, arow_ref, block, head, heads, causal)).astype(bf16)
            y = y + dot(m, xl * head_mask(width, head))
        z = z_ref[0, at, :]
        gated = (y + skip * x) * (z * sigmoid(z))
        gained_ref[0, at, :] = (gated * gain).astype(bf16)
        sq = gated * gated
        total = sq[:, :128]
        for tile in range(1, width // 128):
            total = total + sq[:, 128 * tile : 128 * (tile + 1)]
        squares[at] += total
        weight = expand(cols, W_COL, heads)
        state = ea[BLOCK - 1 :] * state + dot(bt_ref[block], (weight * x).astype(bf16))
        states_ref[0, block + 1] = state

    @pl.when(pl.program_id(0) == pl.num_programs(0) - 1)
    def _():
        sq_ref[...] = jnp.sum(squares[...], axis=1, keepdims=True)


def gate_grads(part, normed_grad, gained, par, rowcols, width):
    z = part[:, :width].astype(f32)
    gain = par[5:6, width:]
    gated = gained.astype(f32) * (1.0 / gain)
    grad = rowcols[:, 0:1] * (normed_grad.astype(f32) * gain) - rowcols[:, 1:2] * gated
    sz = sigmoid(z)
    return grad, z * sz, sz * (1.0 + z * (1.0 - sz))


def back_state_kernel(
    width, z_ref, ngrad_ref, gated_ref, par_ref, cols_ref, row_ref, ct_ref,
    dstate_ref, gain_ref, weighted,
):
    heads = width // HEAD_DIM
    rows = z_ref.shape[1]
    gain_sum = jnp.zeros((8, width), f32)
    for block in range(rows // BLOCK):
        at = pl.ds(block * BLOCK, BLOCK)
        ngrad = ngrad_ref[0, at, :]
        gated = gated_ref[0, at, :]
        grad, silu_z, _ = gate_grads(
            z_ref[0, at, :], ngrad, gated, par_ref[0], row_ref[at], width
        )
        weight = expand(cols_ref[0, at, :], EADEV_COL, heads)
        weighted[at] = (grad * silu_z * weight).astype(bf16)
        prod = ngrad.astype(f32) * gated.astype(f32) * row_ref[at, 0:1]
        gain_sum = gain_sum + jnp.sum(prod.reshape(BLOCK // 8, 8, width), axis=0)
    dstate_ref[0] = dot(ct_ref[...], weighted[...])
    gain_ref[0] = gain_sum * (1.0 / par_ref[0, 5:6, width:])


def product_terms(left, right):
    lane = lax.broadcasted_iota(jnp.int32, (left.shape[0], 128), 1)
    first = lane < HEAD_DIM
    terms = []
    for pair in range(left.shape[1] // 128):
        tile = slice(128 * pair, 128 * (pair + 1))
        value = left[:, tile]
        other = right[:, tile]
        value_high = value.astype(bf16).astype(f32)
        other_high = other.astype(bf16).astype(f32)
        value_low = value - value_high
        other_low = (other - other_high).astype(bf16)
        turned_high = pltpu.roll(value_high, HEAD_DIM, 1)
        turned_low = pltpu.roll(value_low, HEAD_DIM, 1)
        other_turned = pltpu.roll(other_high, HEAD_DIM, 1)
        for even in (True, False):
            if even:
                one = jnp.where(first, value_high, turned_low)
                two = jnp.where(first, value_high, 0.0)
                both = jnp.where(first, other_high, other_turned)
            else:
                one = jnp.where(first, turned_high, value_low)
                two = jnp.where(first, 0.0, value_high)
                both = jnp.where(first, other_turned, other_high)
            terms.append(
                (
                    jnp.concatenate([one.astype(bf16), two.astype(bf16)], axis=1),
                    jnp.concatenate([both.astype(bf16), other_low], axis=1),
                )
            )
    return terms


def fold_rows(value):
    return jnp.sum(value.reshape(value.shape[0] // 8, 8, value.shape[1]), axis=0)


def backward_kernel(
    width, part_ref, u_ref, halo_ref, ngrad_ref, gained_ref, par_ref, cols_ref, arow_ref, row_ref,
    b_ref, c_ref, ct_ref, states_ref, din_ref,
    dpart_ref, tail_ref, head_ref, sums_ref, dcols_ref, dbc_ref,
    scores, dscores, duext, dbacc, dcacc,
):
    heads = width // HEAD_DIM
    rows = part_ref.shape[1]
    blocks = rows // BLOCK
    step = pl.program_id(0)

    @pl.when(step == 0)
    def _():
        dscores[...] = jnp.zeros_like(dscores)
        dbacc[...] = jnp.zeros_like(dbacc)
        dcacc[...] = jnp.zeros_like(dcacc)
        for block in range(blocks):
            at = block_rows(block)
            scores[block] = exact_dot(c_ref[at], b_ref[at], NT)

    taps = par_ref[0, :, width:]
    skip = par_ref[0, 6:7, width:]
    skip_sum = jnp.zeros((8, width), f32)
    tap_sums = [jnp.zeros((8, width), f32) for _ in range(CONV + 1)]
    causal = causal_mask()
    is_last = lax.broadcasted_iota(jnp.int32, (BLOCK, 1), 0) == BLOCK - 1
    d = din_ref[0]
    duext[rows : rows + 8] = jnp.zeros((8, width), f32)
    for block in range(blocks - 1, -1, -1):
        at = block_rows(block)
        cols = cols_ref[0, at, :]
        part = part_ref[0, at, :]
        grad, silu_z, slope_z = gate_grads(
            part, ngrad_ref[0, at, :], gained_ref[0, at, :], par_ref[0], row_ref[at], width
        )
        u = u_ref[0, at, :]
        su = sigmoid(u)
        x = u * su
        xl = x.astype(bf16)
        dy = grad * silu_z
        dyl = dy.astype(bf16)
        dyt = dy.T.astype(bf16)
        s = states_ref[0, block].astype(bf16)
        dl = d.astype(bf16)
        ea = expand(cols, EA_COL, heads)
        weight = expand(cols, W_COL, heads)
        g = scores[block]
        y = ea * dot(c_ref[at].astype(bf16), s)
        dg = dscores[block]
        terms = product_terms(dy, x)
        dxt = []
        for head in range(heads):
            decay = decay_of(cols, arow_ref, block, head, heads, causal)
            m = (g * decay).astype(bf16)
            y = y + dot(m, xl * head_mask(width, head))
            dg = dg + dot(terms[head][0], terms[head][1], NT) * decay
            dxt.append(dot(dyt[HEAD_DIM * head : HEAD_DIM * (head + 1)], m))
        dscores[block] = dg
        dx = jnp.concatenate(dxt, axis=0).T + weight * dot(b_ref[at].astype(bf16), dl)
        zz = xl.astype(f32) * dx
        da = dyl.astype(f32) * y - zz
        ends = jnp.sum(states_ref[0, block + 1] * d, axis=0, keepdims=True)
        da = da + jnp.where(is_last, ends, 0.0)
        dcols_ref[0, at, :] = head_sums(da, zz, heads)
        edy = (ea * dy).astype(bf16)
        dcacc[at] += dot(edy, s, NT)
        dbacc[at] += dot((weight * x).astype(bf16), dl, NT)
        d = ea[BLOCK - 1 :] * d + dot(ct_ref[block], edy)
        du = (dx + skip * dy) * (su * (1.0 + u * (1.0 - su)))
        duext[at] = du
        skip_sum = skip_sum + fold_rows(dy * x)
        dz = grad * (y + skip * x) * slope_z
        dpart_ref[0, at, :width] = dz.astype(bf16)

        raw = part[:, width:]
        draw = taps[CONV - 1 : CONV] * du
        tap_sums[CONV] = tap_sums[CONV] + fold_rows(du)
        tap_sums[CONV - 1] = tap_sums[CONV - 1] + fold_rows(du * raw)
        for offset in range(CONV - 1):
            ahead = block * BLOCK + CONV - 1 - offset
            shifted = duext[ahead : ahead + BLOCK]
            draw = draw + taps[offset : offset + 1] * shifted
            tap_sums[offset] = tap_sums[offset] + fold_rows(shifted * raw)
        dpart_ref[0, at, width:] = draw.astype(bf16)
        if block == blocks - 1:
            tail_ref[0, :, width:] = draw[BLOCK - 16 :]

    tail_ref[0, :, :width] = dpart_ref[0, rows - 16 : rows, :width].astype(f32)
    first_du = duext[0:8]
    head_ref[0, :, :width] = jnp.zeros((8, width), f32)
    head_ref[0, :, width:] = first_du
    for offset in range(CONV - 1):
        for row in range(CONV - 1 - offset):
            at_halo = 8 - (CONV - 1) + offset + row
            tap_sums[offset] = tap_sums[offset] + jnp.where(
                lax.broadcasted_iota(jnp.int32, (8, 1), 0) == row,
                first_du * halo_ref[0, at_halo : at_halo + 1, width:],
                0.0,
            )
    lines = tap_sums + [jnp.zeros((8, width), f32), skip_sum]
    out_rows = [jnp.sum(line, axis=0, keepdims=True) for line in lines]
    sums_ref[0] = jnp.concatenate(out_rows + [jnp.zeros((1, width), f32)], axis=0)

    @pl.when(step == pl.num_programs(0) - 1)
    def _():
        for block in range(blocks):
            at = block_rows(block)
            dg = dscores[block]
            dbc_ref[at, :STATE] = dbacc[at] + exact_dot(dg.T, c_ref[at])
            dbc_ref[at, STATE:] = dcacc[at] + exact_dot(dg, b_ref[at])


def run_kernels(rows, shards, width, group=0, groups=1):
    heads = width // HEAD_DIM
    steps = shards
    blocks = rows // BLOCK
    chans = width

    def over(rows_here, lanes):
        return pl.BlockSpec((1, rows_here, lanes), lambda i: (i, 0, 0))

    def each(*dims):
        return pl.BlockSpec((1,) + dims, lambda i: (i,) + (0,) * len(dims))

    def whole(*dims):
        return pl.BlockSpec(dims, lambda i: (0,) * len(dims))

    part = over(rows, 2 * width)
    halo = over(8, 2 * width)
    par = over(8, 2 * width)
    chan = over(rows, width)
    group_chan = pl.BlockSpec((1, rows, width), lambda i: (i, 0, group))
    anywhere = pl.BlockSpec(memory_space=pl.ANY)
    cols = each(rows, KINDS * heads)
    arow = each(blocks, heads, BLOCK)
    state = over(STATE, width)
    bc = whole(rows, STATE)
    bct = whole(blocks, STATE, BLOCK)
    bct_flat = whole(STATE, rows)
    rowcols = whole(rows, 2)
    shape = jax.ShapeDtypeStruct
    params = pltpu.CompilerParams(
        dimension_semantics=("arbitrary",), vmem_limit_bytes=56 * 1024 * 1024
    )
    elements = rows * shards * chans

    def cost(per_element, reads):
        return pl.CostEstimate(
            flops=elements * per_element, bytes_accessed=elements * reads, transcendentals=0
        )

    x_only = pl.BlockSpec((1, rows, width), lambda i: (i, 0, 1))
    all_states = each(blocks + 1, STATE, width)
    local_state = pl.pallas_call(
        functools.partial(state_kernel, width),
        grid=(steps,),
        in_specs=[x_only, halo, par, cols, bct_flat],
        out_specs=[state, chan],
        out_shape=[shape((shards, STATE, chans), f32), shape((shards, rows, chans), f32)],
        scratch_shapes=[pltpu.VMEM((rows + 8, width), f32), pltpu.VMEM((rows, width), bf16)],
        compiler_params=params,
        cost_estimate=cost(7000, 8),
        name="local_state",
    )
    forward = pl.pallas_call(
        functools.partial(forward_kernel, width),
        grid=(steps,),
        in_specs=[chan, chan, par, cols, arow, bc, bc, bct, state] + [anywhere] * (group > 0),
        out_specs=[group_chan, whole(rows, 1), all_states],
        input_output_aliases={9: 0} if group else {},
        out_shape=[
            shape((shards, rows, groups * chans), bf16),
            shape((rows, 1), f32),
            shape((shards, blocks + 1, STATE, chans), f32),
        ],
        scratch_shapes=[
            pltpu.VMEM((blocks, BLOCK, BLOCK), f32),
            pltpu.VMEM((rows, 128), f32),
        ],
        compiler_params=params,
        cost_estimate=cost(17000, 10),
        name="forward_scan",
    )
    back_state = pl.pallas_call(
        functools.partial(back_state_kernel, width),
        grid=(steps,),
        in_specs=[chan, group_chan, group_chan, par, cols, rowcols, bct_flat],
        out_specs=[state, over(8, width)],
        out_shape=[shape((shards, STATE, chans), f32), shape((shards, 8, chans), f32)],
        scratch_shapes=[pltpu.VMEM((rows, width), bf16)],
        compiler_params=params,
        cost_estimate=cost(8000, 14),
        name="back_state",
    )
    backward = pl.pallas_call(
        functools.partial(backward_kernel, width),
        grid=(steps,),
        in_specs=[
            part, chan, halo, group_chan, group_chan, par, cols, arow, rowcols, bc, bc, bct, all_states,
            state,
        ],
        out_specs=[
            part, over(16, 2 * width), over(8, 2 * width), over(8, width),
            each(rows, 2 * heads), whole(rows, 2 * STATE),
        ],
        out_shape=[
            shape((shards, rows, 2 * chans), bf16),
            shape((shards, 16, 2 * chans), f32),
            shape((shards, 8, 2 * chans), f32),
            shape((shards, 8, chans), f32),
            shape((steps, rows, 2 * heads), f32),
            shape((rows, 2 * STATE), f32),
        ],
        scratch_shapes=[
            pltpu.VMEM((blocks, BLOCK, BLOCK), f32),
            pltpu.VMEM((blocks, BLOCK, BLOCK), f32),
            pltpu.VMEM((rows + 8, width), f32),
            pltpu.VMEM((rows, STATE), f32),
            pltpu.VMEM((rows, STATE), f32),
        ],
        compiler_params=params,
        cost_estimate=cost(43000, 20),
        name="backward_scan",
    )
    return local_state, forward, back_state, backward


def after(value, *others):
    def body(*refs):
        del refs

    anywhere = pl.BlockSpec(memory_space=pl.ANY)
    return pl.pallas_call(
        body,
        in_specs=[anywhere] * (1 + len(others)),
        out_specs=anywhere,
        out_shape=jax.ShapeDtypeStruct(value.shape, value.dtype),
        input_output_aliases={0: 0},
        name="after",
    )(value, *others)


def mp_scatter(array, hold):
    devices = lax.axis_size("mp")
    me = lax.axis_index("mp")
    dims = devices.bit_length() - 1
    array = array.reshape((2,) * dims + array.shape[1:])
    hold = list(hold)
    for bit in range(dims):
        axis = dims - 1 - bit
        upper = lax.rem(lax.div(me, 1 << bit), 2)
        keep = lax.dynamic_index_in_dim(array, upper, axis, keepdims=False)
        give = lax.dynamic_index_in_dim(array, 1 - upper, axis, keepdims=False)
        got = lax.ppermute(give, "mp", [(i, i ^ (1 << bit)) for i in range(devices)])
        ahead = hold.pop(0) if hold else None
        if ahead is not None:
            got = after(got, ahead)
        array = keep + got
    return array


def dp_gather(array, *meanwhile):
    size = lax.axis_size("dp")
    me = lax.axis_index("dp")
    rows = array.shape[0]
    full = jnp.zeros((size * rows,) + array.shape[1:], array.dtype)
    full = lax.dynamic_update_slice(full, array, (me * rows, 0))
    for k in range(1, size):
        got = lax.ppermute(array, "dp", [(i, (i + k) % size) for i in range(size)])
        if meanwhile:
            got = after(got, *meanwhile)
        full = lax.dynamic_update_slice(full, got, (lax.rem(me - k + size, size) * rows, 0))
    return full


def dp_scatter(array, *meanwhile):
    size = lax.axis_size("dp")
    me = lax.axis_index("dp")
    part = array.shape[-1] // size
    total = lax.dynamic_slice_in_dim(array, me * part, part, array.ndim - 1).astype(f32)
    for k in range(1, size):
        there = lax.rem(me + k, size)
        piece = lax.dynamic_slice_in_dim(array, there * part, part, array.ndim - 1)
        got = lax.ppermute(piece, "dp", [(i, (i + k) % size) for i in range(size)])
        if meanwhile:
            got = after(got, *meanwhile)
        total = total + got.astype(f32)
    return total


def exchange_states(carry, totals, reverse, *hold):
    span, own, result, result_log = carry
    devices = lax.axis_size("mp")
    place = lax.div(lax.axis_index("mp"), span)
    shards, _, chans = own.shape

    def over_channels(logs):
        per_chan = jnp.repeat(logs.reshape(shards, 1, -1), HEAD_DIM, axis=-1)
        return jnp.exp(per_chan)

    got = lax.ppermute(own.astype(bf16), "mp", [(i, i ^ span) for i in range(devices)])
    if hold:
        got = after(got, *hold)
    got = got.astype(f32)
    group_logs = totals.reshape(devices // span, span, -1).sum(axis=1)
    high = lax.rem(place, 2) == 1
    nearer = jnp.logical_not(high) if reverse else high
    mine_log = lax.dynamic_index_in_dim(group_logs, place, 0, keepdims=False)
    their_log = lax.dynamic_index_in_dim(
        group_logs, lax.bitwise_xor(place, 1), 0, keepdims=False
    )
    result = result + jnp.where(nearer, over_channels(result_log), 0.0) * got
    result_log = result_log + jnp.where(nearer, their_log, 0.0)
    if 2 * span < devices:
        own = jnp.where(nearer, 1.0, over_channels(their_log)) * own
        own = own + jnp.where(nearer, over_channels(mine_log), 1.0) * got
    return 2 * span, own, result, result_log


def carried_states(own, totals, reverse, hold=(), until=None):
    carry = (1, own, jnp.zeros_like(own), jnp.zeros_like(totals[0]))
    hold = list(hold)
    while carry[0] < (until or lax.axis_size("mp")):
        carry = exchange_states(carry, totals, reverse, *(hold.pop(0) if hold else ()))
    return carry


def causal_filter(extended, taps, rows):
    result = taps[CONV]
    for offset in range(CONV):
        begin = 8 - (CONV - 1) + offset
        result = result + taps[offset] * extended[begin : begin + rows]
    return result


def adam_rows(weight_now, gradient, moments, decayed):
    first_moment = beta_one * moments[0] + (1.0 - beta_one) * gradient
    second_moment = beta_two * moments[1] + (1.0 - beta_two) * gradient * gradient
    direction = (
        first_moment
        / (1.0 - beta_one**STEP)
        / (jnp.sqrt(second_moment / (1.0 - beta_two**STEP)) + adam_eps)
    )
    if decayed:
        direction = direction + decay_rate * weight_now
    return jnp.stack([first_moment, second_moment, direction])


def local(
    tokens,
    cotangent,
    lengths,
    inner_weight,
    step_weight,
    state_weight,
    output_weight,
    inner_filter,
    state_filter,
    head_params,
    norm_gain,
    inner_moments,
    step_moments,
    state_moments,
    output_moments,
    inner_filter_moments,
    state_filter_moments,
    head_moments,
    gain_moments,
):
    shards = lax.axis_size("mp")
    mine = lax.axis_index("mp")
    rows, model = tokens.shape
    own_model, heads_here, _ = inner_weight.shape
    chans = heads_here * HEAD_DIM
    width = min(256, chans)
    step_heads = width // HEAD_DIM
    groups = chans // width
    heads = shards * heads_here
    blocks = rows // BLOCK
    onward = [(i, i + 1) for i in range(shards - 1)]
    homeward = [(i + 1, i) for i in range(shards - 1)]
    kernels = [run_kernels(rows, shards, width, group, groups) for group in range(groups)]

    inner_groups = inner_weight.reshape(own_model, groups, step_heads, 2, HEAD_DIM)
    inner_groups = inner_groups.astype(bf16).transpose(1, 0, 3, 2, 4)
    inner_groups = inner_groups.reshape(groups, own_model, 2 * width)

    packed = jnp.concatenate(
        [
            inner_filter,
            norm_gain[None],
            jnp.repeat(head_params[2], HEAD_DIM)[None],
            jnp.pad(head_params[:2].reshape(1, -1), ((0, 0), (0, chans - 2 * heads_here))),
        ],
        axis=0,
    )
    own_lines = packed.shape[0]
    packed = jnp.concatenate([packed, step_weight.reshape(-1, chans)], axis=0)
    packed = lax.all_gather(packed, "mp", axis=0)
    head_rows = packed[:, 7, : 2 * heads_here].reshape(shards, 2, heads_here)
    step_bias = head_rows[:, 0].reshape(heads)
    decay_base = jnp.exp(head_rows[:, 1].reshape(heads))
    step_all = packed[:, own_lines:].reshape(shards, own_model, heads_here)
    step_all = step_all.astype(bf16).transpose(1, 0, 2).reshape(own_model, heads)
    packed = packed[:, :own_lines]
    params = []
    for group in range(groups):
        here = packed[:, :, group * width : (group + 1) * width]
        params.append(jnp.concatenate([jnp.zeros_like(here), here], axis=-1))

    small_own = jnp.concatenate([step_all, state_weight.astype(bf16)], axis=1)
    inner_low = [dp_gather(inner_groups[0])]
    small = dp_gather(after(small_own, inner_low[0]))

    raw_small = jnp.dot(tokens, small, preferred_element_type=f32)
    state_raw = raw_small[:, heads:]
    state_halo = lax.ppermute(state_raw[rows - 8 :], "mp", onward)
    state_ext = jnp.concatenate([state_halo, state_raw], axis=0)
    state_u = causal_filter(state_ext, state_filter, rows)
    state_sig = jax.nn.sigmoid(state_u)
    state_signal = state_u * state_sig
    writer = state_signal[:, :STATE]
    reader = state_signal[:, STATE:]
    writer_t = writer.T.astype(bf16)
    reader_t = reader.T.astype(bf16)
    writer_blocks = writer_t.reshape(STATE, blocks, BLOCK).transpose(1, 0, 2)
    reader_blocks = reader_t.reshape(STATE, blocks, BLOCK).transpose(1, 0, 2)
    step_arg = raw_small[:, :heads] + step_bias
    step_sizes = jax.nn.softplus(step_arg)
    log_decay = -step_sizes * decay_base
    lower = (jnp.arange(BLOCK)[:, None] >= jnp.arange(BLOCK)[None, :]).astype(f32)
    cumulative = jnp.einsum(
        "ts,bsh->bth", lower, log_decay.reshape(blocks, BLOCK, heads), precision=highest
    )
    block_total = cumulative[:, -1]
    running = jnp.cumsum(block_total, axis=0)
    before = running - block_total
    device_total = running[-1]
    dt_blocks = step_sizes.reshape(blocks, BLOCK, heads)
    from_start = cumulative + before[:, None]
    kinds = [
        cumulative,
        jnp.exp(cumulative),
        jnp.exp(block_total[:, None] - cumulative) * dt_blocks,
        jnp.exp(device_total - from_start) * dt_blocks,
        jnp.exp(from_start),
    ]
    by_group = (shards, groups, step_heads)
    columns = jnp.stack(kinds).reshape((KINDS, rows) + by_group)
    columns = [
        columns[:, :, :, group].transpose(2, 1, 0, 3).reshape(shards, rows, KINDS * step_heads)
        for group in range(groups)
    ]
    arows = (cumulative - jnp.log(dt_blocks)).reshape((blocks, BLOCK) + by_group)
    arows = arows.transpose(3, 2, 0, 4, 1)

    totals_all = lax.all_gather(device_total, "mp", axis=0)
    totals_groups = totals_all.reshape((shards,) + by_group).transpose(2, 0, 1, 3)
    totals_groups = totals_groups.reshape(groups, shards, shards * step_heads)

    for group in range(1, groups):
        inner_low.append(dp_gather(after(inner_groups[group], small), columns[0], totals_all))
    inner_full = [lax.all_gather(own, "mp", axis=0) for own in inner_low]
    parts, halos, all_states, all_u, gained_before = [], [], [], [], []
    squares = 0.0
    ready = [columns[0]]
    for group in range(groups):
        inner_full[group] = after(inner_full[group], *ready)
        part = jnp.einsum(
            "td,mdc->mtc", tokens, inner_full[group], preferred_element_type=f32
        )
        halo = lax.ppermute(part[:, rows - 8 :], "mp", onward)
        if group == 0:
            out_low = dp_gather(after(output_weight.astype(bf16), inner_low[-1]), halo)
            out_full = lax.all_gather(out_low, "mp", axis=0)
            halo = after(halo, out_low)
        ends, u = kernels[group][0](part, halo, params[group], columns[group], writer_t)
        state_in = carried_states(ends, totals_groups[group], False)[2]
        gained, sq, states = kernels[group][1](
            part, u, params[group], columns[group], arows[group], writer, reader,
            writer_blocks, state_in, *gained_before,
        )
        gained_before = [gained]
        squares = squares + sq
        ready = [states]
        parts.append(part)
        halos.append(halo)
        all_states.append(states)
        all_u.append(u)
    norm_scale = lax.rsqrt(squares / INNER + eps_norm)
    branch = norm_scale * jnp.einsum(
        "mtc,mdc->td", gained, out_full, preferred_element_type=f32
    )
    positions = mine * rows + jnp.arange(rows)
    live = (positions < lengths[0]).astype(f32)[:, None]
    mixed = (tokens.astype(f32) + live * branch).astype(bf16)

    masked = (cotangent.astype(f32) * live).astype(bf16)
    scaled_sum = jnp.sum(masked.astype(f32) * branch, axis=1, keepdims=True)
    row_columns = jnp.concatenate(
        [norm_scale, norm_scale * norm_scale * scaled_sum / INNER], axis=1
    )
    normed_grad = jnp.einsum("td,mdc->mtc", masked, out_full, preferred_element_type=f32)
    starts, gain_sums = [], []
    for group in range(groups):
        start, gain_sum = kernels[group][2](
            parts[group], normed_grad, gained, params[group], columns[group],
            after(row_columns, *starts), reader_t,
        )
        starts.append(start)
        gain_sums.append(gain_sum)
    scaled_cot = after((masked.astype(f32) * norm_scale).astype(bf16), starts[-1])
    out_part = jnp.einsum(
        "td,mtc->mcd", scaled_cot, gained, preferred_element_type=f32
    ).astype(bf16)
    out_sum = lax.psum_scatter(out_part, "mp", scatter_dimension=0)
    carries = []
    for group in range(groups):
        hold = [starts[1:], [out_part]] if group == 0 else [[out_part]]
        until = shards if group == 0 else shards // 2
        carries.append(carried_states(starts[group], totals_groups[group], True, hold, until))
    waiting = [carry[1] for carry in carries[1:]] + [out_part]
    dparts, inner_sums, dbc, all_sums, all_dcols = [], [], 0.0, [], []
    for group in range(groups):
        carry = carries[group]
        if group:
            carry = exchange_states(carry, totals_groups[group], True, dw_part)
        dpart, tail, du_head, sums, dcols, dbc_here = kernels[group][3](
            parts[group], all_u[group], halos[group], normed_grad, gained,
            params[group], columns[group], arows[group], row_columns, writer, reader,
            reader_blocks, all_states[group], after(carry[2], *waiting),
        )
        du_next = lax.ppermute(du_head, "mp", homeward)
        extra = [
            sum(params[group][:, k] * du_next[:, i - k] for k in range(i + 1))
            for i in range(CONV - 1)
        ]
        extra = jnp.concatenate(
            [jnp.zeros((shards, 13, 2 * width), f32), jnp.stack(extra, axis=1)], axis=1
        )
        dpart = lax.dynamic_update_slice(
            dpart, (tail + extra).astype(bf16), (0, rows - 16, 0)
        )
        inner_part = jnp.einsum("td,mtc->mcd", tokens, dpart, preferred_element_type=f32)
        inner_part = dw_part = inner_part.astype(bf16)
        if group == 0:
            out_sum = after(out_sum, dcols).reshape(chans, -1, own_model).transpose(1, 0, 2)
            out_sum = lax.psum_scatter(out_sum, "dp", scatter_dimension=0)
            inner_part = after(inner_part, out_sum)
        inner_part = after(inner_part, *inner_sums)
        inner_sums.append(lax.psum_scatter(inner_part, "mp", scatter_dimension=0))
        waiting = [inner_part] + ([out_sum] if group == groups - 2 else [])
        dparts.append(dpart)
        dbc = dbc + dbc_here
        all_sums.append(sums)
        all_dcols.append(dcols)
    dbc = after(dbc, inner_part)
    all_dcols[-1] = after(all_dcols[-1], inner_part)

    dcols = jnp.stack(all_dcols).reshape(groups, shards, rows, 2, step_heads)
    dcols = dcols.transpose(3, 2, 1, 0, 4).reshape(2, rows, heads)
    dlog = jnp.einsum(
        "st,bsh->bth", lower, dcols[0].reshape(blocks, BLOCK, heads), precision=highest
    ).reshape(rows, heads)
    slope = jax.nn.sigmoid(step_arg)
    ratio = jnp.where(step_sizes > 1e-20, slope / jnp.maximum(step_sizes, 1e-20), 1.0)
    dstep = dcols[1] * ratio - dlog * decay_base * slope
    sums = jnp.concatenate(all_sums, axis=-1)
    gains = jnp.concatenate(gain_sums, axis=-1)
    head_line = jnp.concatenate(
        [
            jnp.sum(dstep, axis=0).reshape(shards, heads_here),
            jnp.sum(dlog * log_decay, axis=0).reshape(shards, heads_here),
            jnp.sum(sums[:, 6].reshape(shards, heads_here, HEAD_DIM), axis=-1),
        ],
        axis=1,
    )
    head_line = jnp.pad(head_line, ((0, 0), (0, chans - 3 * heads_here)))[:, None]
    du_state = dbc * (state_sig * (1.0 + state_u * (1.0 - state_sig)))
    du_state_next = lax.ppermute(du_state[:8], "mp", homeward)
    du_state_ext = jnp.concatenate([du_state, du_state_next], axis=0)
    dstate_raw = sum(
        state_filter[k] * du_state_ext[CONV - 1 - k : CONV - 1 - k + rows] for k in range(CONV)
    )
    state_filter_part = jnp.stack(
        [jnp.sum(du_state * state_ext[5 + k : 5 + k + rows], axis=0) for k in range(CONV)]
        + [jnp.sum(du_state, axis=0)]
    )
    dsmall = jnp.concatenate([dstep, dstate_raw], axis=1).astype(bf16)

    small_grad = lax.dot_general(
        dsmall, tokens, (((0,), (0,)), ((), ())), preferred_element_type=f32
    )
    state_share = 2 * STATE // shards
    lines = -(-(CONV + 1) * 2 * STATE // chans)
    filter_lines = jnp.pad(
        state_filter_part.reshape(-1), (0, lines * chans - (CONV + 1) * 2 * STATE)
    )
    filter_lines = jnp.broadcast_to(filter_lines.reshape(1, lines, chans), (shards, lines, chans))
    sums_here = jnp.concatenate(
        [sums[:, : CONV + 1], jnp.sum(gains, axis=1, keepdims=True), head_line, filter_lines],
        axis=1,
    ).reshape(shards, -1)
    sum_rows = -(-sums_here.shape[1] // model)
    sum_size = sums_here.shape[1]
    sums_here = jnp.pad(sums_here, ((0, 0), (0, sum_rows * model - sum_size)))
    small_grad = jnp.concatenate(
        [
            small_grad[:heads].reshape(shards, heads_here, model),
            small_grad[heads:].reshape(shards, state_share, model),
            sums_here.reshape(shards, sum_rows, model),
        ],
        axis=1,
    )
    small_rows = heads_here + state_share
    def input_gradient(group, *others):
        return jnp.einsum(
            "mtc,mdc->td", after(dparts[group], *others), inner_full[group],
            preferred_element_type=f32,
        )

    input_parts = [input_gradient(group, small_grad) for group in range(groups - 1)]
    output_gradient = after(out_sum, *input_parts).astype(f32).T
    output_update = adam_rows(output_weight, output_gradient, output_moments, True)
    inner_grads = [
        dp_scatter(after(total, *input_parts), output_update) for total in inner_sums[:-1]
    ]
    small_total = mp_scatter(small_grad, input_parts + [output_update])
    small_part = lax.dot_general(dsmall, small, (NT, ((), ())), preferred_element_type=f32)
    last_sum = inner_sums[-1].reshape(2 * width, -1, own_model).transpose(1, 0, 2)
    input_parts.append(input_gradient(groups - 1, small_total, last_sum))
    tokens_gradient = sum(input_parts) + (cotangent.astype(f32) + small_part)
    tokens_gradient = tokens_gradient.astype(bf16)
    last_sum = lax.psum_scatter(last_sum, "dp", scatter_dimension=0)
    inner_grads.append(last_sum.astype(f32))

    dp_size = lax.axis_size("dp")
    dp_mine = lax.axis_index("dp")
    sum_lines = small_total[small_rows:].reshape(-1, own_model)

    def share(owner):
        piece = lax.dynamic_slice_in_dim(small_total[:small_rows], owner * own_model, own_model, 1)
        return jnp.concatenate([piece, sum_lines], axis=0)

    small_sum = share(dp_mine)
    for k in range(1, dp_size):
        got = lax.ppermute(
            share(lax.rem(dp_mine + k, dp_size)), "dp",
            [(i, (i + k) % dp_size) for i in range(dp_size)],
        )
        small_sum = small_sum + after(got, tokens_gradient)
    own = small_sum[small_rows:].reshape(-1)[:sum_size].reshape(-1, chans)
    step_gradient = small_sum[:heads_here].T
    state_gradient = lax.all_gather(small_sum[heads_here:small_rows], "mp", axis=0, tiled=True).T
    inner_gradient = jnp.stack(inner_grads)
    inner_gradient = inner_gradient.reshape(groups, 2, step_heads, HEAD_DIM, own_model)
    inner_gradient = inner_gradient.transpose(4, 0, 2, 1, 3)
    inner_gradient = inner_gradient.reshape(own_model, heads_here, 2 * HEAD_DIM)
    state_filter_gradient = own[CONV + 3 :].reshape(-1)[: (CONV + 1) * 2 * STATE]
    state_filter_gradient = state_filter_gradient.reshape(CONV + 1, 2 * STATE)
    inner_filter_gradient = own[: CONV + 1]
    gain_gradient = own[CONV + 1]
    head_gradient = own[CONV + 2, : 3 * heads_here].reshape(3, heads_here)

    inner_update = adam_rows(inner_weight, inner_gradient, inner_moments, True)
    step_update = adam_rows(step_weight, step_gradient, step_moments, True)
    state_update = adam_rows(state_weight, state_gradient, state_moments, True)
    inner_filter_update = adam_rows(inner_filter, inner_filter_gradient, inner_filter_moments, True)
    state_filter_update = adam_rows(state_filter, state_filter_gradient, state_filter_moments, True)
    head_update = adam_rows(head_params, head_gradient, head_moments, False)
    gain_update = adam_rows(norm_gain, gain_gradient, gain_moments, False)
    return (
        mixed,
        tokens_gradient,
        inner_gradient,
        step_gradient,
        state_gradient,
        output_gradient,
        inner_filter_gradient,
        state_filter_gradient,
        head_gradient,
        gain_gradient,
        inner_update,
        step_update,
        state_update,
        output_update,
        inner_filter_update,
        state_filter_update,
        head_update,
        gain_update,
    )


def solution(mesh):
    return jax.shard_map(
        local,
        mesh=mesh,
        in_specs=(
            P(("dp", "mp"), None),
            P(("dp", "mp"), None),
            P("dp"),
            P("dp", "mp", None),
            P("dp", "mp"),
            P("dp", None),
            P("dp", "mp"),
            P(None, "mp"),
            P(),
            P(None, "mp"),
            P("mp"),
            P(None, "dp", "mp", None),
            P(None, "dp", "mp"),
            P(None, "dp", None),
            P(None, "dp", "mp"),
            P(None, None, "mp"),
            P(),
            P(None, None, "mp"),
            P(None, "mp"),
        ),
        out_specs=(
            P(("dp", "mp"), None),
            P(("dp", "mp"), None),
            P("dp", "mp", None),
            P("dp", "mp"),
            P("dp", None),
            P("dp", "mp"),
            P(None, "mp"),
            P(),
            P(None, "mp"),
            P("mp"),
            P(None, "dp", "mp", None),
            P(None, "dp", "mp"),
            P(None, "dp", None),
            P(None, "dp", "mp"),
            P(None, None, "mp"),
            P(),
            P(None, None, "mp"),
            P(None, "mp"),
        ),
        check_vma=False,
    )
```

```python
import functools

import jax
import jax.numpy as jnp
from jax import lax
from jax.experimental import pallas as pl
from jax.experimental.pallas import tpu as pltpu
from jax.sharding import PartitionSpec as P

HEAD_DIM = 64
STATE = 128
CONV = 4
BLOCK = 256
STEP = 100
INNER = 4096

highest = lax.Precision.HIGHEST
eps_norm = 1e-05
beta_one = 0.9
beta_two = 0.95
adam_eps = 1e-08
decay_rate = 0.1

f32 = jnp.float32
bf16 = jnp.bfloat16

KINDS = 5
A_COL, EA_COL, W_COL, WDEV_COL, EADEV_COL = range(KINDS)


def dot(left, right, dims=((1,), (0,))):
    return lax.dot_general(left, right, (dims, ((), ())), preferred_element_type=f32)


NT = ((1,), (1,))


def exact_dot(left, right, dims=((1,), (0,))):
    return lax.dot_general(
        left, right, (dims, ((), ())), precision=highest, preferred_element_type=f32
    )


def sigmoid(value):
    return 1.0 / (1.0 + jnp.exp(-value))


def expand(cols, kind, heads):
    rows = cols.shape[0]
    first = lax.broadcasted_iota(jnp.int32, (rows, 128), 1) < HEAD_DIM
    tiles = []
    for pair in range(heads // 2):
        at = kind * heads + 2 * pair
        tiles.append(jnp.where(first, cols[:, at : at + 1], cols[:, at + 1 : at + 2]))
    return tiles[0] if len(tiles) == 1 else jnp.concatenate(tiles, axis=1)


def head_sums(one, two, heads):
    width = one.shape[1]
    lanes = lax.broadcasted_iota(jnp.int32, (width, 2 * heads), 0) // HEAD_DIM
    places = lax.broadcasted_iota(jnp.int32, (width, 2 * heads), 1)
    pick_one = jnp.where(lanes == places, 1.0, 0.0).astype(bf16)
    pick_two = jnp.where(lanes + heads == places, 1.0, 0.0).astype(bf16)
    one_high = one.astype(bf16)
    two_high = two.astype(bf16)
    one_low = (one - one_high.astype(f32)).astype(bf16)
    two_low = (two - two_high.astype(f32)).astype(bf16)
    return (dot(one_high, pick_one) + dot(one_low, pick_one)) + (
        dot(two_high, pick_two) + dot(two_low, pick_two)
    )


def head_mask(width, head):
    lanes = lax.broadcasted_iota(jnp.int32, (1, width), 1)
    return jnp.where(lanes // HEAD_DIM == head, 1.0, 0.0).astype(bf16)


def block_rows(index):
    return pl.ds(index * BLOCK, BLOCK)


def filtered(extended, taps, base):
    result = taps[CONV : CONV + 1]
    for offset in range(CONV):
        begin = base + 8 - (CONV - 1) + offset
        result = result + taps[offset : offset + 1] * extended[begin : begin + BLOCK]
    return result


def decay_of(cols_block, arow_ref, block, head, heads, causal):
    column = cols_block[:, A_COL * heads + head : A_COL * heads + head + 1]
    row = arow_ref[0, block, head : head + 1, :]
    return jnp.exp(jnp.where(causal, column - row, -jnp.inf))


def causal_mask():
    rows = lax.broadcasted_iota(jnp.int32, (BLOCK, BLOCK), 0)
    return rows >= lax.broadcasted_iota(jnp.int32, (BLOCK, BLOCK), 1)


def state_kernel(
    width, x_ref, halo_ref, par_ref, cols_ref, bt_ref, state_ref, u_ref, xext, weighted
):
    heads = width // HEAD_DIM
    rows = x_ref.shape[1]
    xext[0:8] = halo_ref[0, :, width:]
    xext[8 : 8 + rows] = x_ref[0]
    taps = par_ref[0, :, width:]
    for block in range(rows // BLOCK):
        at = pl.ds(block * BLOCK, BLOCK)
        u = filtered(xext, taps, block * BLOCK)
        u_ref[0, at, :] = u
        weight = expand(cols_ref[0, at, :], WDEV_COL, heads)
        weighted[at] = (u * sigmoid(u) * weight).astype(bf16)
    state_ref[0] = dot(bt_ref[...], weighted[...])


def forward_kernel(
    width, z_ref, u_ref, par_ref, cols_ref, arow_ref, b_ref, c_ref, bt_ref, sin_ref, *rest
):
    gained_ref, sq_ref, states_ref, scores, squares = rest[-5:]
    heads = width // HEAD_DIM
    rows = z_ref.shape[1]
    blocks = rows // BLOCK

    @pl.when(pl.program_id(0) == 0)
    def _():
        squares[...] = jnp.zeros_like(squares)
        for block in range(blocks):
            at = block_rows(block)
            scores[block] = exact_dot(c_ref[at], b_ref[at], NT)

    gain = par_ref[0, 5:6, width:]
    skip = par_ref[0, 6:7, width:]
    causal = causal_mask()
    state = sin_ref[0]
    states_ref[0, 0] = state
    for block in range(blocks):
        at = block_rows(block)
        cols = cols_ref[0, at, :]
        u = u_ref[0, at, :]
        x = u * sigmoid(u)
        xl = x.astype(bf16)
        ea = expand(cols, EA_COL, heads)
        y = ea * dot(c_ref[at].astype(bf16), state.astype(bf16))
        g = scores[block]
        for head in range(heads):
            m = (g * decay_of(cols, arow_ref, block, head, heads, causal)).astype(bf16)
            y = y + dot(m, xl * head_mask(width, head))
        z = z_ref[0, at, :]
        gated = (y + skip * x) * (z * sigmoid(z))
        gained_ref[0, at, :] = (gated * gain).astype(bf16)
        sq = gated * gated
        total = sq[:, :128]
        for tile in range(1, width // 128):
            total = total + sq[:, 128 * tile : 128 * (tile + 1)]
        squares[at] += total
        weight = expand(cols, W_COL, heads)
        state = ea[BLOCK - 1 :] * state + dot(bt_ref[block], (weight * x).astype(bf16))
        states_ref[0, block + 1] = state

    @pl.when(pl.program_id(0) == pl.num_programs(0) - 1)
    def _():
        sq_ref[...] = jnp.sum(squares[...], axis=1, keepdims=True)


def gate_grads(part, normed_grad, gained, par, rowcols, width):
    z = part[:, :width].astype(f32)
    gain = par[5:6, width:]
    gated = gained.astype(f32) * (1.0 / gain)
    grad = rowcols[:, 0:1] * (normed_grad.astype(f32) * gain) - rowcols[:, 1:2] * gated
    sz = sigmoid(z)
    return grad, z * sz, sz * (1.0 + z * (1.0 - sz))


def back_state_kernel(
    width, z_ref, ngrad_ref, gated_ref, par_ref, cols_ref, row_ref, ct_ref,
    dstate_ref, gain_ref, weighted,
):
    heads = width // HEAD_DIM
    rows = z_ref.shape[1]
    gain_sum = jnp.zeros((8, width), f32)
    for block in range(rows // BLOCK):
        at = pl.ds(block * BLOCK, BLOCK)
        ngrad = ngrad_ref[0, at, :]
        gated = gated_ref[0, at, :]
        grad, silu_z, _ = gate_grads(
            z_ref[0, at, :], ngrad, gated, par_ref[0], row_ref[at], width
        )
        weight = expand(cols_ref[0, at, :], EADEV_COL, heads)
        weighted[at] = (grad * silu_z * weight).astype(bf16)
        prod = ngrad.astype(f32) * gated.astype(f32) * row_ref[at, 0:1]
        gain_sum = gain_sum + jnp.sum(prod.reshape(BLOCK // 8, 8, width), axis=0)
    dstate_ref[0] = dot(ct_ref[...], weighted[...])
    gain_ref[0] = gain_sum * (1.0 / par_ref[0, 5:6, width:])


def product_terms(left, right):
    lane = lax.broadcasted_iota(jnp.int32, (left.shape[0], 128), 1)
    first = lane < HEAD_DIM
    terms = []
    for pair in range(left.shape[1] // 128):
        tile = slice(128 * pair, 128 * (pair + 1))
        value = left[:, tile]
        other = right[:, tile]
        value_high = value.astype(bf16).astype(f32)
        other_high = other.astype(bf16).astype(f32)
        value_low = value - value_high
        other_low = (other - other_high).astype(bf16)
        turned_high = pltpu.roll(value_high, HEAD_DIM, 1)
        turned_low = pltpu.roll(value_low, HEAD_DIM, 1)
        other_turned = pltpu.roll(other_high, HEAD_DIM, 1)
        for even in (True, False):
            if even:
                one = jnp.where(first, value_high, turned_low)
                two = jnp.where(first, value_high, 0.0)
                both = jnp.where(first, other_high, other_turned)
            else:
                one = jnp.where(first, turned_high, value_low)
                two = jnp.where(first, 0.0, value_high)
                both = jnp.where(first, other_turned, other_high)
            terms.append(
                (
                    jnp.concatenate([one.astype(bf16), two.astype(bf16)], axis=1),
                    jnp.concatenate([both.astype(bf16), other_low], axis=1),
                )
            )
    return terms


def fold_rows(value):
    return jnp.sum(value.reshape(value.shape[0] // 8, 8, value.shape[1]), axis=0)


def backward_kernel(
    width, part_ref, u_ref, halo_ref, ngrad_ref, gained_ref, par_ref, cols_ref, arow_ref, row_ref,
    b_ref, c_ref, ct_ref, states_ref, din_ref,
    dpart_ref, tail_ref, head_ref, sums_ref, dcols_ref, dbc_ref,
    scores, dscores, duext, dbacc, dcacc,
):
    heads = width // HEAD_DIM
    rows = part_ref.shape[1]
    blocks = rows // BLOCK
    step = pl.program_id(0)

    @pl.when(step == 0)
    def _():
        dscores[...] = jnp.zeros_like(dscores)
        dbacc[...] = jnp.zeros_like(dbacc)
        dcacc[...] = jnp.zeros_like(dcacc)
        for block in range(blocks):
            at = block_rows(block)
            scores[block] = exact_dot(c_ref[at], b_ref[at], NT)

    taps = par_ref[0, :, width:]
    skip = par_ref[0, 6:7, width:]
    skip_sum = jnp.zeros((8, width), f32)
    tap_sums = [jnp.zeros((8, width), f32) for _ in range(CONV + 1)]
    causal = causal_mask()
    is_last = lax.broadcasted_iota(jnp.int32, (BLOCK, 1), 0) == BLOCK - 1
    d = din_ref[0]
    duext[rows : rows + 8] = jnp.zeros((8, width), f32)
    for block in range(blocks - 1, -1, -1):
        at = block_rows(block)
        cols = cols_ref[0, at, :]
        part = part_ref[0, at, :]
        grad, silu_z, slope_z = gate_grads(
            part, ngrad_ref[0, at, :], gained_ref[0, at, :], par_ref[0], row_ref[at], width
        )
        u = u_ref[0, at, :]
        su = sigmoid(u)
        x = u * su
        xl = x.astype(bf16)
        dy = grad * silu_z
        dyl = dy.astype(bf16)
        dyt = dy.T.astype(bf16)
        s = states_ref[0, block].astype(bf16)
        dl = d.astype(bf16)
        ea = expand(cols, EA_COL, heads)
        weight = expand(cols, W_COL, heads)
        g = scores[block]
        y = ea * dot(c_ref[at].astype(bf16), s)
        dg = dscores[block]
        terms = product_terms(dy, x)
        dxt = []
        for head in range(heads):
            decay = decay_of(cols, arow_ref, block, head, heads, causal)
            m = (g * decay).astype(bf16)
            y = y + dot(m, xl * head_mask(width, head))
            dg = dg + dot(terms[head][0], terms[head][1], NT) * decay
            dxt.append(dot(dyt[HEAD_DIM * head : HEAD_DIM * (head + 1)], m))
        dscores[block] = dg
        dx = jnp.concatenate(dxt, axis=0).T + weight * dot(b_ref[at].astype(bf16), dl)
        zz = xl.astype(f32) * dx
        da = dyl.astype(f32) * y - zz
        ends = jnp.sum(states_ref[0, block + 1] * d, axis=0, keepdims=True)
        da = da + jnp.where(is_last, ends, 0.0)
        dcols_ref[0, at, :] = head_sums(da, zz, heads)
        edy = (ea * dy).astype(bf16)
        dcacc[at] += dot(edy, s, NT)
        dbacc[at] += dot((weight * x).astype(bf16), dl, NT)
        d = ea[BLOCK - 1 :] * d + dot(ct_ref[block], edy)
        du = (dx + skip * dy) * (su * (1.0 + u * (1.0 - su)))
        duext[at] = du
        skip_sum = skip_sum + fold_rows(dy * x)
        dz = grad * (y + skip * x) * slope_z
        dpart_ref[0, at, :width] = dz.astype(bf16)

        raw = part[:, width:]
        draw = taps[CONV - 1 : CONV] * du
        tap_sums[CONV] = tap_sums[CONV] + fold_rows(du)
        tap_sums[CONV - 1] = tap_sums[CONV - 1] + fold_rows(du * raw)
        for offset in range(CONV - 1):
            ahead = block * BLOCK + CONV - 1 - offset
            shifted = duext[ahead : ahead + BLOCK]
            draw = draw + taps[offset : offset + 1] * shifted
            tap_sums[offset] = tap_sums[offset] + fold_rows(shifted * raw)
        dpart_ref[0, at, width:] = draw.astype(bf16)
        if block == blocks - 1:
            tail_ref[0, :, width:] = draw[BLOCK - 16 :]

    tail_ref[0, :, :width] = dpart_ref[0, rows - 16 : rows, :width].astype(f32)
    first_du = duext[0:8]
    head_ref[0, :, :width] = jnp.zeros((8, width), f32)
    head_ref[0, :, width:] = first_du
    for offset in range(CONV - 1):
        for row in range(CONV - 1 - offset):
            at_halo = 8 - (CONV - 1) + offset + row
            tap_sums[offset] = tap_sums[offset] + jnp.where(
                lax.broadcasted_iota(jnp.int32, (8, 1), 0) == row,
                first_du * halo_ref[0, at_halo : at_halo + 1, width:],
                0.0,
            )
    lines = tap_sums + [jnp.zeros((8, width), f32), skip_sum]
    out_rows = [jnp.sum(line, axis=0, keepdims=True) for line in lines]
    sums_ref[0] = jnp.concatenate(out_rows + [jnp.zeros((1, width), f32)], axis=0)

    @pl.when(step == pl.num_programs(0) - 1)
    def _():
        for block in range(blocks):
            at = block_rows(block)
            dg = dscores[block]
            dbc_ref[at, :STATE] = dbacc[at] + exact_dot(dg.T, c_ref[at])
            dbc_ref[at, STATE:] = dcacc[at] + exact_dot(dg, b_ref[at])


def run_kernels(rows, shards, width, group=0, groups=1):
    heads = width // HEAD_DIM
    steps = shards
    blocks = rows // BLOCK
    chans = width

    def over(rows_here, lanes):
        return pl.BlockSpec((1, rows_here, lanes), lambda i: (i, 0, 0))

    def each(*dims):
        return pl.BlockSpec((1,) + dims, lambda i: (i,) + (0,) * len(dims))

    def whole(*dims):
        return pl.BlockSpec(dims, lambda i: (0,) * len(dims))

    part = over(rows, 2 * width)
    halo = over(8, 2 * width)
    par = over(8, 2 * width)
    chan = over(rows, width)
    group_chan = pl.BlockSpec((1, rows, width), lambda i: (i, 0, group))
    anywhere = pl.BlockSpec(memory_space=pl.ANY)
    cols = each(rows, KINDS * heads)
    arow = each(blocks, heads, BLOCK)
    state = over(STATE, width)
    bc = whole(rows, STATE)
    bct = whole(blocks, STATE, BLOCK)
    bct_flat = whole(STATE, rows)
    rowcols = whole(rows, 2)
    shape = jax.ShapeDtypeStruct
    params = pltpu.CompilerParams(
        dimension_semantics=("arbitrary",), vmem_limit_bytes=56 * 1024 * 1024
    )
    elements = rows * shards * chans

    def cost(per_element, reads):
        return pl.CostEstimate(
            flops=elements * per_element, bytes_accessed=elements * reads, transcendentals=0
        )

    x_only = pl.BlockSpec((1, rows, width), lambda i: (i, 0, 1))
    all_states = each(blocks + 1, STATE, width)
    local_state = pl.pallas_call(
        functools.partial(state_kernel, width),
        grid=(steps,),
        in_specs=[x_only, halo, par, cols, bct_flat],
        out_specs=[state, chan],
        out_shape=[shape((shards, STATE, chans), f32), shape((shards, rows, chans), f32)],
        scratch_shapes=[pltpu.VMEM((rows + 8, width), f32), pltpu.VMEM((rows, width), bf16)],
        compiler_params=params,
        cost_estimate=cost(7000, 8),
        name="local_state",
    )
    forward = pl.pallas_call(
        functools.partial(forward_kernel, width),
        grid=(steps,),
        in_specs=[chan, chan, par, cols, arow, bc, bc, bct, state] + [anywhere] * (group > 0),
        out_specs=[group_chan, whole(rows, 1), all_states],
        input_output_aliases={9: 0} if group else {},
        out_shape=[
            shape((shards, rows, groups * chans), bf16),
            shape((rows, 1), f32),
            shape((shards, blocks + 1, STATE, chans), f32),
        ],
        scratch_shapes=[
            pltpu.VMEM((blocks, BLOCK, BLOCK), f32),
            pltpu.VMEM((rows, 128), f32),
        ],
        compiler_params=params,
        cost_estimate=cost(17000, 10),
        name="forward_scan",
    )
    back_state = pl.pallas_call(
        functools.partial(back_state_kernel, width),
        grid=(steps,),
        in_specs=[chan, group_chan, group_chan, par, cols, rowcols, bct_flat],
        out_specs=[state, over(8, width)],
        out_shape=[shape((shards, STATE, chans), f32), shape((shards, 8, chans), f32)],
        scratch_shapes=[pltpu.VMEM((rows, width), bf16)],
        compiler_params=params,
        cost_estimate=cost(8000, 14),
        name="back_state",
    )
    backward = pl.pallas_call(
        functools.partial(backward_kernel, width),
        grid=(steps,),
        in_specs=[
            part, chan, halo, group_chan, group_chan, par, cols, arow, rowcols, bc, bc, bct, all_states,
            state,
        ],
        out_specs=[
            part, over(16, 2 * width), over(8, 2 * width), over(8, width),
            each(rows, 2 * heads), whole(rows, 2 * STATE),
        ],
        out_shape=[
            shape((shards, rows, 2 * chans), bf16),
            shape((shards, 16, 2 * chans), f32),
            shape((shards, 8, 2 * chans), f32),
            shape((shards, 8, chans), f32),
            shape((steps, rows, 2 * heads), f32),
            shape((rows, 2 * STATE), f32),
        ],
        scratch_shapes=[
            pltpu.VMEM((blocks, BLOCK, BLOCK), f32),
            pltpu.VMEM((blocks, BLOCK, BLOCK), f32),
            pltpu.VMEM((rows + 8, width), f32),
            pltpu.VMEM((rows, STATE), f32),
            pltpu.VMEM((rows, STATE), f32),
        ],
        compiler_params=params,
        cost_estimate=cost(43000, 20),
        name="backward_scan",
    )
    return local_state, forward, back_state, backward


def after(value, *others):
    def body(*refs):
        del refs

    anywhere = pl.BlockSpec(memory_space=pl.ANY)
    return pl.pallas_call(
        body,
        in_specs=[anywhere] * (1 + len(others)),
        out_specs=anywhere,
        out_shape=jax.ShapeDtypeStruct(value.shape, value.dtype),
        input_output_aliases={0: 0},
        name="after",
    )(value, *others)


def mp_scatter(array, hold):
    devices = lax.axis_size("mp")
    me = lax.axis_index("mp")
    dims = devices.bit_length() - 1
    array = array.reshape((2,) * dims + array.shape[1:])
    hold = list(hold)
    for bit in range(dims):
        axis = dims - 1 - bit
        upper = lax.rem(lax.div(me, 1 << bit), 2)
        keep = lax.dynamic_index_in_dim(array, upper, axis, keepdims=False)
        give = lax.dynamic_index_in_dim(array, 1 - upper, axis, keepdims=False)
        got = lax.ppermute(give, "mp", [(i, i ^ (1 << bit)) for i in range(devices)])
        ahead = hold.pop(0) if hold else None
        if ahead is not None:
            got = after(got, ahead)
        array = keep + got
    return array


def dp_gather(array, *meanwhile):
    size = lax.axis_size("dp")
    me = lax.axis_index("dp")
    rows = array.shape[0]
    full = jnp.zeros((size * rows,) + array.shape[1:], array.dtype)
    full = lax.dynamic_update_slice(full, array, (me * rows, 0))
    for k in range(1, size):
        got = lax.ppermute(array, "dp", [(i, (i + k) % size) for i in range(size)])
        if meanwhile:
            got = after(got, *meanwhile)
        full = lax.dynamic_update_slice(full, got, (lax.rem(me - k + size, size) * rows, 0))
    return full


def dp_scatter(array, *meanwhile):
    size = lax.axis_size("dp")
    me = lax.axis_index("dp")
    part = array.shape[-1] // size
    total = lax.dynamic_slice_in_dim(array, me * part, part, array.ndim - 1).astype(f32)
    for k in range(1, size):
        there = lax.rem(me + k, size)
        piece = lax.dynamic_slice_in_dim(array, there * part, part, array.ndim - 1)
        got = lax.ppermute(piece, "dp", [(i, (i + k) % size) for i in range(size)])
        if meanwhile:
            got = after(got, *meanwhile)
        total = total + got.astype(f32)
    return total


def exchange_states(carry, totals, reverse, *hold):
    span, own, result, result_log = carry
    devices = lax.axis_size("mp")
    place = lax.div(lax.axis_index("mp"), span)
    shards, _, chans = own.shape

    def over_channels(logs):
        per_chan = jnp.repeat(logs.reshape(shards, 1, -1), HEAD_DIM, axis=-1)
        return jnp.exp(per_chan)

    got = lax.ppermute(own.astype(bf16), "mp", [(i, i ^ span) for i in range(devices)])
    if hold:
        got = after(got, *hold)
    got = got.astype(f32)
    group_logs = totals.reshape(devices // span, span, -1).sum(axis=1)
    high = lax.rem(place, 2) == 1
    nearer = jnp.logical_not(high) if reverse else high
    mine_log = lax.dynamic_index_in_dim(group_logs, place, 0, keepdims=False)
    their_log = lax.dynamic_index_in_dim(
        group_logs, lax.bitwise_xor(place, 1), 0, keepdims=False
    )
    result = result + jnp.where(nearer, over_channels(result_log), 0.0) * got
    result_log = result_log + jnp.where(nearer, their_log, 0.0)
    if 2 * span < devices:
        own = jnp.where(nearer, 1.0, over_channels(their_log)) * own
        own = own + jnp.where(nearer, over_channels(mine_log), 1.0) * got
    return 2 * span, own, result, result_log


def carried_states(own, totals, reverse, hold=(), until=None):
    carry = (1, own, jnp.zeros_like(own), jnp.zeros_like(totals[0]))
    hold = list(hold)
    while carry[0] < (until or lax.axis_size("mp")):
        carry = exchange_states(carry, totals, reverse, *(hold.pop(0) if hold else ()))
    return carry


def causal_filter(extended, taps, rows):
    result = taps[CONV]
    for offset in range(CONV):
        begin = 8 - (CONV - 1) + offset
        result = result + taps[offset] * extended[begin : begin + rows]
    return result


def adam_rows(weight_now, gradient, moments, decayed):
    first_moment = beta_one * moments[0] + (1.0 - beta_one) * gradient
    second_moment = beta_two * moments[1] + (1.0 - beta_two) * gradient * gradient
    direction = (
        first_moment
        / (1.0 - beta_one**STEP)
        / (jnp.sqrt(second_moment / (1.0 - beta_two**STEP)) + adam_eps)
    )
    if decayed:
        direction = direction + decay_rate * weight_now
    return jnp.stack([first_moment, second_moment, direction])


def adam_step(weight_now, gradient, first_moment, second_moment):
    first_moment = beta_one * first_moment + (1.0 - beta_one) * gradient
    second_moment = beta_two * second_moment + (1.0 - beta_two) * gradient * gradient
    direction = (
        first_moment
        / (1.0 - beta_one**STEP)
        / (jnp.sqrt(second_moment / (1.0 - beta_two**STEP)) + adam_eps)
    )
    return first_moment, second_moment, direction + decay_rate * weight_now


def inner_update_kernel(step_heads, *refs):
    sums = refs[:-4]
    weight_ref, moments_ref, grad_ref, update_ref = refs[-4:]
    width = step_heads * HEAD_DIM
    for head in range(weight_ref.shape[1]):
        total = sums[head // step_heads]
        begin = head % step_heads * HEAD_DIM
        gate = total[begin : begin + HEAD_DIM].astype(f32)
        signal = total[width + begin : width + begin + HEAD_DIM].astype(f32)
        grad_ref[:, head, :] = jnp.concatenate([gate, signal], axis=0).T
    results = adam_step(weight_ref[...], grad_ref[...], moments_ref[0], moments_ref[1])
    for place, result in enumerate(results):
        update_ref[place] = result


def update_inner(totals, weight, moments, step_heads):
    rows, heads, lanes = weight.shape
    tile = 128
    flat = pl.BlockSpec((tile, heads, lanes), lambda i: (i, 0, 0))
    stacked = [pl.BlockSpec((n, tile, heads, lanes), lambda i: (0, i, 0, 0)) for n in (2, 3)]
    return pl.pallas_call(
        functools.partial(inner_update_kernel, step_heads),
        grid=(rows // tile,),
        in_specs=[pl.BlockSpec((total.shape[0], tile), lambda i: (0, i)) for total in totals]
        + [flat, stacked[0]],
        out_specs=[flat, stacked[1]],
        out_shape=[
            jax.ShapeDtypeStruct(weight.shape, f32),
            jax.ShapeDtypeStruct((3,) + weight.shape, f32),
        ],
        compiler_params=pltpu.CompilerParams(vmem_limit_bytes=40 * 1024 * 1024),
        name="inner_update",
    )(*totals, weight, moments)


def output_update_kernel(total_ref, weight_ref, moments_ref, grad_ref, update_ref):
    gradient = total_ref[...].astype(f32).T
    grad_ref[...] = gradient
    results = adam_step(weight_ref[...], gradient, moments_ref[0], moments_ref[1])
    for place, result in enumerate(results):
        update_ref[place] = result


def update_output(total, weight, moments):
    rows, columns = weight.shape
    tile = 128
    flat = pl.BlockSpec((tile, columns), lambda i: (i, 0))
    stacked = [pl.BlockSpec((n, tile, columns), lambda i: (0, i, 0)) for n in (2, 3)]
    return pl.pallas_call(
        output_update_kernel,
        grid=(rows // tile,),
        in_specs=[pl.BlockSpec((columns, tile), lambda i: (0, i)), flat, stacked[0]],
        out_specs=[flat, stacked[1]],
        out_shape=[
            jax.ShapeDtypeStruct(weight.shape, f32),
            jax.ShapeDtypeStruct((3,) + weight.shape, f32),
        ],
        compiler_params=pltpu.CompilerParams(vmem_limit_bytes=40 * 1024 * 1024),
        name="output_update",
    )(total, weight, moments)


def local(
    tokens,
    cotangent,
    lengths,
    inner_weight,
    step_weight,
    state_weight,
    output_weight,
    inner_filter,
    state_filter,
    head_params,
    norm_gain,
    inner_moments,
    step_moments,
    state_moments,
    output_moments,
    inner_filter_moments,
    state_filter_moments,
    head_moments,
    gain_moments,
):
    shards = lax.axis_size("mp")
    mine = lax.axis_index("mp")
    rows, model = tokens.shape
    own_model, heads_here, _ = inner_weight.shape
    chans = heads_here * HEAD_DIM
    width = min(256, chans)
    step_heads = width // HEAD_DIM
    groups = chans // width
    heads = shards * heads_here
    blocks = rows // BLOCK
    onward = [(i, i + 1) for i in range(shards - 1)]
    homeward = [(i + 1, i) for i in range(shards - 1)]
    kernels = [run_kernels(rows, shards, width, group, groups) for group in range(groups)]

    inner_groups = inner_weight.reshape(own_model, groups, step_heads, 2, HEAD_DIM)
    inner_groups = inner_groups.astype(bf16).transpose(1, 0, 3, 2, 4)
    inner_groups = inner_groups.reshape(groups, own_model, 2 * width)

    packed = jnp.concatenate(
        [
            inner_filter,
            norm_gain[None],
            jnp.repeat(head_params[2], HEAD_DIM)[None],
            jnp.pad(head_params[:2].reshape(1, -1), ((0, 0), (0, chans - 2 * heads_here))),
        ],
        axis=0,
    )
    own_lines = packed.shape[0]
    packed = jnp.concatenate([packed, step_weight.reshape(-1, chans)], axis=0)
    packed = lax.all_gather(packed, "mp", axis=0)
    head_rows = packed[:, 7, : 2 * heads_here].reshape(shards, 2, heads_here)
    step_bias = head_rows[:, 0].reshape(heads)
    decay_base = jnp.exp(head_rows[:, 1].reshape(heads))
    step_all = packed[:, own_lines:].reshape(shards, own_model, heads_here)
    step_all = step_all.astype(bf16).transpose(1, 0, 2).reshape(own_model, heads)
    packed = packed[:, :own_lines]
    params = []
    for group in range(groups):
        here = packed[:, :, group * width : (group + 1) * width]
        params.append(jnp.concatenate([jnp.zeros_like(here), here], axis=-1))

    small_own = jnp.concatenate([step_all, state_weight.astype(bf16)], axis=1)
    inner_low = [dp_gather(inner_groups[0])]
    small = dp_gather(after(small_own, inner_low[0]))

    raw_small = jnp.dot(tokens, small, preferred_element_type=f32)
    state_raw = raw_small[:, heads:]
    state_halo = lax.ppermute(state_raw[rows - 8 :], "mp", onward)
    state_ext = jnp.concatenate([state_halo, state_raw], axis=0)
    state_u = causal_filter(state_ext, state_filter, rows)
    state_sig = jax.nn.sigmoid(state_u)
    state_signal = state_u * state_sig
    writer = state_signal[:, :STATE]
    reader = state_signal[:, STATE:]
    writer_t = writer.T.astype(bf16)
    reader_t = reader.T.astype(bf16)
    writer_blocks = writer_t.reshape(STATE, blocks, BLOCK).transpose(1, 0, 2)
    reader_blocks = reader_t.reshape(STATE, blocks, BLOCK).transpose(1, 0, 2)
    step_arg = raw_small[:, :heads] + step_bias
    step_sizes = jax.nn.softplus(step_arg)
    log_decay = -step_sizes * decay_base
    lower = (jnp.arange(BLOCK)[:, None] >= jnp.arange(BLOCK)[None, :]).astype(f32)
    cumulative = jnp.einsum(
        "ts,bsh->bth", lower, log_decay.reshape(blocks, BLOCK, heads), precision=highest
    )
    block_total = cumulative[:, -1]
    running = jnp.cumsum(block_total, axis=0)
    before = running - block_total
    device_total = running[-1]
    dt_blocks = step_sizes.reshape(blocks, BLOCK, heads)
    from_start = cumulative + before[:, None]
    kinds = [
        cumulative,
        jnp.exp(cumulative),
        jnp.exp(block_total[:, None] - cumulative) * dt_blocks,
        jnp.exp(device_total - from_start) * dt_blocks,
        jnp.exp(from_start),
    ]
    by_group = (shards, groups, step_heads)
    columns = jnp.stack(kinds).reshape((KINDS, rows) + by_group)
    columns = [
        columns[:, :, :, group].transpose(2, 1, 0, 3).reshape(shards, rows, KINDS * step_heads)
        for group in range(groups)
    ]
    arows = (cumulative - jnp.log(dt_blocks)).reshape((blocks, BLOCK) + by_group)
    arows = arows.transpose(3, 2, 0, 4, 1)

    totals_all = lax.all_gather(device_total, "mp", axis=0)
    totals_groups = totals_all.reshape((shards,) + by_group).transpose(2, 0, 1, 3)
    totals_groups = totals_groups.reshape(groups, shards, shards * step_heads)

    for group in range(1, groups):
        inner_low.append(dp_gather(after(inner_groups[group], small), columns[0], totals_all))
    inner_full = [lax.all_gather(own, "mp", axis=0) for own in inner_low]
    parts, halos, all_states, all_u, gained_before = [], [], [], [], []
    squares = 0.0
    ready = [columns[0]]
    for group in range(groups):
        inner_full[group] = after(inner_full[group], *ready)
        part = jnp.einsum(
            "td,mdc->mtc", tokens, inner_full[group], preferred_element_type=f32
        )
        halo = lax.ppermute(part[:, rows - 8 :], "mp", onward)
        if group == 0:
            out_low = dp_gather(after(output_weight.astype(bf16), inner_low[-1]), halo)
            out_full = lax.all_gather(out_low, "mp", axis=0)
            halo = after(halo, out_low)
        ends, u = kernels[group][0](part, halo, params[group], columns[group], writer_t)
        state_in = carried_states(ends, totals_groups[group], False)[2]
        gained, sq, states = kernels[group][1](
            part, u, params[group], columns[group], arows[group], writer, reader,
            writer_blocks, state_in, *gained_before,
        )
        gained_before = [gained]
        squares = squares + sq
        ready = [states]
        parts.append(part)
        halos.append(halo)
        all_states.append(states)
        all_u.append(u)
    norm_scale = lax.rsqrt(squares / INNER + eps_norm)
    positions = mine * rows + jnp.arange(rows)
    live = (positions < lengths[0]).astype(f32)[:, None]
    masked = (cotangent.astype(f32) * live).astype(bf16)
    scaled_cot = (masked.astype(f32) * norm_scale).astype(bf16)
    out_part = jnp.einsum(
        "td,mtc->mcd", scaled_cot, gained, preferred_element_type=f32
    ).astype(bf16)
    out_sum = lax.psum_scatter(out_part, "mp", scatter_dimension=0)

    normed_grad = jnp.einsum(
        "td,mdc->mtc", after(masked, out_part), out_full, preferred_element_type=f32
    )
    inner_sum = jnp.sum(normed_grad * gained.astype(f32), axis=(0, 2))[:, None]
    row_columns = jnp.concatenate([norm_scale, norm_scale**3 * inner_sum / INNER], axis=1)
    starts, gain_sums = [], []
    for group in range(groups):
        start, gain_sum = kernels[group][2](
            parts[group], normed_grad, gained, params[group], columns[group],
            after(row_columns, *starts), reader_t,
        )
        starts.append(start)
        gain_sums.append(gain_sum)

    branch = norm_scale * jnp.einsum(
        "mtc,mdc->td", gained, after(out_full, *starts), preferred_element_type=f32
    )
    mixed = (tokens.astype(f32) + live * branch).astype(bf16)
    carries = []
    for group in range(groups):
        hold = [starts[1:], [mixed]] if group == 0 else [[mixed]]
        until = shards if group == 0 else shards // 2
        carries.append(carried_states(starts[group], totals_groups[group], True, hold, until))
    waiting = [carry[1] for carry in carries[1:]] + [mixed]
    dparts, inner_sums, dbc, all_sums, all_dcols = [], [], 0.0, [], []
    for group in range(groups):
        carry = carries[group]
        if group:
            carry = exchange_states(carry, totals_groups[group], True, inner_part)
        dpart, tail, du_head, sums, dcols, dbc_here = kernels[group][3](
            parts[group], all_u[group], halos[group], normed_grad, gained,
            params[group], columns[group], arows[group], row_columns, writer, reader,
            reader_blocks, all_states[group], after(carry[2], *waiting),
        )
        du_next = lax.ppermute(du_head, "mp", homeward)
        extra = [
            sum(params[group][:, k] * du_next[:, i - k] for k in range(i + 1))
            for i in range(CONV - 1)
        ]
        extra = jnp.concatenate(
            [jnp.zeros((shards, 13, 2 * width), f32), jnp.stack(extra, axis=1)], axis=1
        )
        dpart = lax.dynamic_update_slice(
            dpart, (tail + extra).astype(bf16), (0, rows - 16, 0)
        )
        inner_part = jnp.einsum("td,mtc->mcd", tokens, dpart, preferred_element_type=f32)
        if group == 0:
            out_sum = after(out_sum, dcols).reshape(chans, -1, own_model).transpose(1, 0, 2)
            out_sum = lax.psum_scatter(out_sum, "dp", scatter_dimension=0)
        inner_part = after(inner_part.astype(bf16), *(inner_sums or [out_sum]))
        inner_sums.append(lax.psum_scatter(inner_part, "mp", scatter_dimension=0))
        waiting = [inner_part]
        dparts.append(dpart)
        dbc = dbc + dbc_here
        all_sums.append(sums)
        all_dcols.append(dcols)
    dbc = after(dbc, inner_part)
    all_dcols[-1] = after(all_dcols[-1], inner_part)

    dcols = jnp.stack(all_dcols).reshape(groups, shards, rows, 2, step_heads)
    dcols = dcols.transpose(3, 2, 1, 0, 4).reshape(2, rows, heads)
    dlog = jnp.einsum(
        "st,bsh->bth", lower, dcols[0].reshape(blocks, BLOCK, heads), precision=highest
    ).reshape(rows, heads)
    slope = jax.nn.sigmoid(step_arg)
    ratio = jnp.where(step_sizes > 1e-20, slope / jnp.maximum(step_sizes, 1e-20), 1.0)
    dstep = dcols[1] * ratio - dlog * decay_base * slope
    sums = jnp.concatenate(all_sums, axis=-1)
    gains = jnp.concatenate(gain_sums, axis=-1)
    head_line = jnp.concatenate(
        [
            jnp.sum(dstep, axis=0).reshape(shards, heads_here),
            jnp.sum(dlog * log_decay, axis=0).reshape(shards, heads_here),
            jnp.sum(sums[:, 6].reshape(shards, heads_here, HEAD_DIM), axis=-1),
        ],
        axis=1,
    )
    head_line = jnp.pad(head_line, ((0, 0), (0, chans - 3 * heads_here)))[:, None]
    du_state = dbc * (state_sig * (1.0 + state_u * (1.0 - state_sig)))
    du_state_next = lax.ppermute(du_state[:8], "mp", homeward)
    du_state_ext = jnp.concatenate([du_state, du_state_next], axis=0)
    dstate_raw = sum(
        state_filter[k] * du_state_ext[CONV - 1 - k : CONV - 1 - k + rows] for k in range(CONV)
    )
    state_filter_part = jnp.stack(
        [jnp.sum(du_state * state_ext[5 + k : 5 + k + rows], axis=0) for k in range(CONV)]
        + [jnp.sum(du_state, axis=0)]
    )
    dsmall = jnp.concatenate([dstep, dstate_raw], axis=1).astype(bf16)

    small_grad = lax.dot_general(
        dsmall, tokens, (((0,), (0,)), ((), ())), preferred_element_type=f32
    )
    state_share = 2 * STATE // shards
    lines = -(-(CONV + 1) * 2 * STATE // chans)
    filter_lines = jnp.pad(
        state_filter_part.reshape(-1), (0, lines * chans - (CONV + 1) * 2 * STATE)
    )
    filter_lines = jnp.broadcast_to(filter_lines.reshape(1, lines, chans), (shards, lines, chans))
    sums_here = jnp.concatenate(
        [sums[:, : CONV + 1], jnp.sum(gains, axis=1, keepdims=True), head_line, filter_lines],
        axis=1,
    ).reshape(shards, -1)
    sum_rows = -(-sums_here.shape[1] // model)
    sum_size = sums_here.shape[1]
    sums_here = jnp.pad(sums_here, ((0, 0), (0, sum_rows * model - sum_size)))
    small_grad = jnp.concatenate(
        [
            small_grad[:heads].reshape(shards, heads_here, model),
            small_grad[heads:].reshape(shards, state_share, model),
            sums_here.reshape(shards, sum_rows, model),
        ],
        axis=1,
    )
    small_rows = heads_here + state_share
    def input_gradient(group, *others):
        return jnp.einsum(
            "mtc,mdc->td", after(dparts[group], *others), inner_full[group],
            preferred_element_type=f32,
        )

    input_parts = [input_gradient(group, small_grad) for group in range(groups - 1)]
    inner_grads = [dp_scatter(total, *input_parts) for total in inner_sums[:-1]]
    output_gradient, output_update = update_output(
        after(out_sum, *input_parts, *inner_grads), output_weight, output_moments
    )
    last_sum = inner_sums[-1].reshape(2 * width, -1, own_model).transpose(1, 0, 2)
    small_total = mp_scatter(small_grad, [None] + input_parts[:1] + [output_update])
    small_part = lax.dot_general(dsmall, small, (NT, ((), ())), preferred_element_type=f32)
    input_parts.append(input_gradient(groups - 1, small_total, last_sum))
    tokens_gradient = sum(input_parts) + (cotangent.astype(f32) + small_part)
    tokens_gradient = tokens_gradient.astype(bf16)
    last_sum = lax.psum_scatter(last_sum, "dp", scatter_dimension=0)
    inner_grads.append(last_sum)

    dp_size = lax.axis_size("dp")
    dp_mine = lax.axis_index("dp")
    sum_lines = small_total[small_rows:].reshape(-1, own_model)

    def share(owner):
        piece = lax.dynamic_slice_in_dim(small_total[:small_rows], owner * own_model, own_model, 1)
        return jnp.concatenate([piece, sum_lines], axis=0)

    small_sum = share(dp_mine)
    for k in range(1, dp_size):
        got = lax.ppermute(
            share(lax.rem(dp_mine + k, dp_size)), "dp",
            [(i, (i + k) % dp_size) for i in range(dp_size)],
        )
        small_sum = small_sum + after(got, tokens_gradient)
    own = small_sum[small_rows:].reshape(-1)[:sum_size].reshape(-1, chans)
    step_gradient = small_sum[:heads_here].T
    state_gradient = lax.all_gather(small_sum[heads_here:small_rows], "mp", axis=0, tiled=True).T
    inner_gradient, inner_update = update_inner(
        inner_grads, inner_weight, inner_moments, step_heads
    )
    state_filter_gradient = own[CONV + 3 :].reshape(-1)[: (CONV + 1) * 2 * STATE]
    state_filter_gradient = state_filter_gradient.reshape(CONV + 1, 2 * STATE)
    inner_filter_gradient = own[: CONV + 1]
    gain_gradient = own[CONV + 1]
    head_gradient = own[CONV + 2, : 3 * heads_here].reshape(3, heads_here)

    step_update = adam_rows(step_weight, step_gradient, step_moments, True)
    state_update = adam_rows(state_weight, state_gradient, state_moments, True)
    inner_filter_update = adam_rows(inner_filter, inner_filter_gradient, inner_filter_moments, True)
    state_filter_update = adam_rows(state_filter, state_filter_gradient, state_filter_moments, True)
    head_update = adam_rows(head_params, head_gradient, head_moments, False)
    gain_update = adam_rows(norm_gain, gain_gradient, gain_moments, False)
    return (
        mixed,
        tokens_gradient,
        inner_gradient,
        step_gradient,
        state_gradient,
        output_gradient,
        inner_filter_gradient,
        state_filter_gradient,
        head_gradient,
        gain_gradient,
        inner_update,
        step_update,
        state_update,
        output_update,
        inner_filter_update,
        state_filter_update,
        head_update,
        gain_update,
    )


def solution(mesh):
    return jax.shard_map(
        local,
        mesh=mesh,
        in_specs=(
            P(("dp", "mp"), None),
            P(("dp", "mp"), None),
            P("dp"),
            P("dp", "mp", None),
            P("dp", "mp"),
            P("dp", None),
            P("dp", "mp"),
            P(None, "mp"),
            P(),
            P(None, "mp"),
            P("mp"),
            P(None, "dp", "mp", None),
            P(None, "dp", "mp"),
            P(None, "dp", None),
            P(None, "dp", "mp"),
            P(None, None, "mp"),
            P(),
            P(None, None, "mp"),
            P(None, "mp"),
        ),
        out_specs=(
            P(("dp", "mp"), None),
            P(("dp", "mp"), None),
            P("dp", "mp", None),
            P("dp", "mp"),
            P("dp", None),
            P("dp", "mp"),
            P(None, "mp"),
            P(),
            P(None, "mp"),
            P("mp"),
            P(None, "dp", "mp", None),
            P(None, "dp", "mp"),
            P(None, "dp", None),
            P(None, "dp", "mp"),
            P(None, None, "mp"),
            P(),
            P(None, None, "mp"),
            P(None, "mp"),
        ),
        check_vma=False,
    )
```
